256 devices in a mesh: row: 16 (over z, x_hi), col: 16 (over y, x_lo, core).
Axes of the slice: x: 4 (x_hi: 2, x_lo: 2; x = x_hi * 2 + x_lo), y: 4, z: 8, core: 2. Of those that a mesh axis runs over, the one named last changes fastest.
Arguments:
- affinity_tiles: bfloat16 [16, 16, 80, 128, 128], P('row', 'col'), may hold values from -14983200 to 14983200, as said below
- tile_index: int32 [16, 16, 2, 80], P('row', 'col'), may hold values from 0 to 15, as said below
- start_block: bfloat16 [32768, 128], P(('row', 'col')), may hold values from -6 to 6
Outputs:
- ritz_block: float32 [32768, 128], P(('row', 'col'))
- ritz_gram: float32 [128, 128], replicated
The draws below stay inside these ranges and needn't reach their ends.
Inputs may be any that keep to these rules, and one draw needn't show every extreme that they name: `tile_index`: each device's slots name distinct tiles of its block; the tile pattern of A is symmetric and holds every diagonal tile; slots without a tile carry indices 0 and 0 and a zero tile. `affinity_tiles`: A is symmetric: the tile at tile row I and tile column J is the transpose of the tile at J and I; every diagonal entry of A is 1 or more.
All inputs are finite; a program needn't handle non-finite values.
Results may differ from the reference program's by a relative error of at most 0.00115.
The reference program's roundings to bfloat16 on the way count: a program that leaves them out, or rounds other values in their place, can miss the bound.
Values may be sent and summed in bfloat16 or wider, within the bound.
A program may use at most 64 MiB of HBM per device.

```python
import jax
import jax.numpy as jnp
from jax import lax

TILE = 128
VECS = 128
TPD = 1
POWER = 3
TILES = 256
ORDER = 32768
SLOTS = 80
N_ROW = 16
N_COL = 16


def tile_pattern(key):
    supers = N_ROW * N_COL
    key_turn, key_place = jax.random.split(key)
    rotation = jax.random.randint(key_turn, (supers // 4,), 0, 4)
    labels = jnp.arange(supers, dtype=jnp.int32)
    residue = (labels % 4 + rotation[labels // 4]) % 4
    position = jax.random.randint(key_place, (supers, supers), 0, TPD * TPD)
    inner = jnp.arange(TPD, dtype=jnp.int32)

    def block(row_id, col_id):
        source = row_id * N_COL + jnp.arange(N_COL, dtype=jnp.int32)
        target = col_id * N_ROW + jnp.arange(N_ROW, dtype=jnp.int32)
        upper = source[:, None]
        lefty = target[None, :]
        linked = (upper != lefty) & ((residue[upper] + residue[lefty]) % 4 == 0)
        place = position[jnp.minimum(upper, lefty), jnp.maximum(upper, lefty)]
        first = place // TPD
        second = place % TPD
        inner_row = jnp.where(upper < lefty, first, second)
        inner_col = jnp.where(upper < lefty, second, first)
        cell_row = (upper - row_id * N_COL) * TPD + inner_row
        cell_col = (lefty - col_id * N_ROW) * TPD + inner_col
        diag_row = (source[:, None] - row_id * N_COL) * TPD + inner[None, :]
        diag_col = (source[:, None] - col_id * N_ROW) * TPD + inner[None, :]
        diag_live = (source >= col_id * N_ROW) & (source < (col_id + 1) * N_ROW)
        diag_live = jnp.broadcast_to(diag_live[:, None], (N_COL, TPD))
        all_rows = jnp.concatenate([cell_row.reshape(-1), diag_row.reshape(-1)])
        all_cols = jnp.concatenate([cell_col.reshape(-1), diag_col.reshape(-1)])
        all_live = jnp.concatenate([linked.reshape(-1), diag_live.reshape(-1)])
        ranking = jnp.argsort(jnp.where(all_live, 0, 1).astype(jnp.int32), stable=True)[:SLOTS]
        keeper = all_live[ranking]
        rows_kept = jnp.where(keeper, all_rows[ranking], 0).astype(jnp.int32)
        cols_kept = jnp.where(keeper, all_cols[ranking], 0).astype(jnp.int32)
        return (rows_kept, cols_kept, keeper)
    row_ids = jnp.arange(N_ROW, dtype=jnp.int32)
    col_ids = jnp.arange(N_COL, dtype=jnp.int32)
    return jax.vmap(lambda one_row: jax.vmap(lambda one_col: block(one_row, one_col))(col_ids))(row_ids)


def draw_tile_index(key, part):
    rows_kept, cols_kept, keeper = tile_pattern(key)
    return jnp.stack([rows_kept, cols_kept], axis=2).astype(jnp.int32)


def draw_affinity_tiles(key, part):
    rows_kept, cols_kept, keeper = tile_pattern(key)
    key = jax.random.fold_in(key, 7)
    key_scale, key_value = jax.random.split(key)
    weights = jnp.exp(jax.random.uniform(key_scale, (ORDER,), jnp.float32, 0.0, jnp.log(10.0)))
    dominance = 2.0 * jnp.sqrt(jnp.float32(TILE * (N_ROW * N_COL // (4 * TPD) + 1)))
    row_base = (jnp.arange(N_ROW, dtype=jnp.int32) * (TPD * N_COL))[:, None, None]
    col_base = (jnp.arange(N_COL, dtype=jnp.int32) * (TPD * N_ROW))[None, :, None]
    global_row = rows_kept + row_base
    global_col = cols_kept + col_base
    identity = jnp.eye(TILE, dtype=jnp.float32)

    def one_tile(tile_row, tile_col, live):
        smaller = jnp.minimum(tile_row, tile_col)
        larger = jnp.maximum(tile_row, tile_col)
        tile_key = jax.random.fold_in(key_value, smaller * TILES + larger)
        values = jnp.clip(jax.random.normal(tile_key, (TILE, TILE), jnp.float32), -4.0, 4.0)
        oriented = jnp.where(tile_row > tile_col, values.T, values)
        mirrored = 0.5 * (values + values.T)
        boosted = mirrored * (1.0 - identity) + identity * (dominance + jnp.abs(mirrored))
        chosen = jnp.where(tile_row == tile_col, boosted, oriented)
        left = lax.dynamic_slice_in_dim(weights, tile_row * TILE, TILE)
        right = lax.dynamic_slice_in_dim(weights, tile_col * TILE, TILE)
        return chosen * left[:, None] * right[None, :] * live.astype(jnp.float32)
    tiles_drawn = jax.vmap(jax.vmap(jax.vmap(one_tile)))(global_row, global_col, keeper)
    return tiles_drawn.astype(jnp.bfloat16)


def shard_levels(own_key, extent, cuts, least, high):
    gain, own = 1.0, jax.random.fold_in(own_key, 6)
    for dim, parts in cuts:
        heights = jnp.exp(jax.random.uniform(jax.random.fold_in(own, dim), (parts,), jnp.float32, least / len(cuts), high / len(cuts)))
        gain = gain * jnp.repeat(heights, extent[dim] // parts).reshape([-1 if axis == dim else 1 for axis in range(len(extent))])
    return gain


def scatter_about(stream_key, dims, width, reach, pieces=(), kind=jnp.bfloat16):
    drawn = jax.random.normal(stream_key, dims, jnp.float32) * width
    if len(pieces) > 0:
        drawn = shard_levels(stream_key, dims, pieces, -0.22, 0.18) * drawn
    return jnp.clip(drawn, min=-reach, max=reach).astype(kind)


def setup_inputs(seed: int = 0) -> dict:
    splits = jax.random.split(jax.random.key(seed), 4)
    affinity_tiles = draw_affinity_tiles(jax.random.fold_in(splits[3], 71), 0)
    tile_index = draw_tile_index(jax.random.fold_in(splits[3], 71), 0)
    start_block = scatter_about(splits[2], (ORDER, VECS), 1.0, 6.0, ((0, 256),))
    return dict(affinity_tiles=affinity_tiles, tile_index=tile_index, start_block=start_block)


def peaks(block, index):
    magnitude = jnp.abs(block.astype(jnp.float32))
    best = jax.ops.segment_max(lax.optimization_barrier(jnp.max(magnitude, axis=2)), index[0], num_segments=TPD * N_COL)
    return jnp.maximum(best, 0.0).reshape(-1)

def product_across(block, index, inputs):
    picked = inputs[index[0]]
    terms = jnp.einsum('sab,sav->sbv', block.astype(jnp.float32), picked.astype(jnp.float32))
    return jax.ops.segment_sum(terms, index[1], num_segments=TPD * N_ROW)

def product_along(block, index, inputs):
    picked = inputs[index[1]]
    terms = jnp.einsum('sab,sbv->sav', block.astype(jnp.float32), picked.astype(jnp.float32))
    return jax.ops.segment_sum(terms, index[0], num_segments=TPD * N_COL)

def across(affinity_tiles, tile_index, weighted):
    blocks = weighted.reshape(N_ROW, TPD * N_COL, TILE, VECS)

    def advance(total, which):
        tiles_row = lax.dynamic_index_in_dim(affinity_tiles, which, 0, keepdims=False)
        index_row = lax.dynamic_index_in_dim(tile_index, which, 0, keepdims=False)
        inputs = lax.dynamic_index_in_dim(blocks, which, 0, keepdims=False)
        partial_value = jax.vmap(product_across, in_axes=(0, 0, None))(tiles_row, index_row, inputs)
        return (total + partial_value, None)
    start = jnp.zeros((N_COL, TPD * N_ROW, TILE, VECS), jnp.float32)
    total, unused = lax.scan(advance, start, jnp.arange(N_ROW, dtype=jnp.int32))
    return total.reshape(ORDER, VECS)

def along(affinity_tiles, tile_index, weighted):
    blocks = weighted.reshape(N_COL, TPD * N_ROW, TILE, VECS)

    def advance(total, which):
        tiles_col = lax.dynamic_index_in_dim(affinity_tiles, which, 1, keepdims=False)
        index_col = lax.dynamic_index_in_dim(tile_index, which, 1, keepdims=False)
        inputs = lax.dynamic_index_in_dim(blocks, which, 0, keepdims=False)
        partial_value = jax.vmap(product_along, in_axes=(0, 0, None))(tiles_col, index_col, inputs)
        return (total + partial_value, None)
    start = jnp.zeros((N_ROW, TPD * N_COL, TILE, VECS), jnp.float32)
    total, unused = lax.scan(advance, start, jnp.arange(N_COL, dtype=jnp.int32))
    return total.reshape(ORDER, VECS)

def reference(affinity_tiles, tile_index, start_block):

    def block_row(which):
        tiles_row = lax.dynamic_index_in_dim(affinity_tiles, which, 0, keepdims=False)
        index_row = lax.dynamic_index_in_dim(tile_index, which, 0, keepdims=False)
        return jax.vmap(peaks)(tiles_row, index_row)
    maxima = lax.map(block_row, jnp.arange(N_ROW, dtype=jnp.int32))
    row_peak = lax.optimization_barrier(jnp.max(maxima, axis=1)).reshape(-1)
    scale = (1.0 / jnp.sqrt(row_peak))[:, None]
    squared = scale * scale
    weighted = (scale * start_block.astype(jnp.float32)).astype(jnp.bfloat16)
    power = None
    for step in range(POWER):
        if step % 2 == 0:
            power = across(affinity_tiles, tile_index, weighted)
        else:
            power = along(affinity_tiles, tile_index, weighted)
        if step + 1 < POWER:
            weighted = (squared * power).astype(jnp.bfloat16)
    iterate = scale * power
    gram = jnp.dot(iterate.T.astype(jnp.float32), iterate.astype(jnp.float32), precision=lax.Precision.HIGHEST, preferred_element_type=jnp.float32) / ORDER
    lower = jnp.linalg.cholesky(gram)
    basis = jax.scipy.linalg.solve_triangular(lower, iterate.T, lower=True).T
    weighted = (scale * basis).astype(jnp.bfloat16)
    ritz_block = scale * along(affinity_tiles, tile_index, weighted)
    ritz_gram = jnp.dot(ritz_block.T.astype(jnp.float32), ritz_block.astype(jnp.float32), precision=lax.Precision.HIGHEST, preferred_element_type=jnp.float32) / ORDER
    return (ritz_block, ritz_gram)
```

```python
import functools

import jax
import jax.numpy as jnp
from jax import lax
from jax.experimental import pallas as pl
from jax.experimental.pallas import tpu as pltpu
from jax.sharding import PartitionSpec as P

EDGE = 128
PANEL = 16
MESH = pl.DeviceIdType.MESH
HIGH = lax.Precision.HIGHEST
F32 = jnp.float32
BF16 = jnp.bfloat16


def kernel(
    nr, nc, slots, order,
    tiles_hbm, table, cell, start_ref,
    ritz_ref, gram_ref,
    tiles, dense, rbuf, cbuf, scale_r, scale_c,
    own_s, own_w, sT, w1, w2, w3, w4,
    parts, lands, gpart, ga, gs, gb, gfull, elim,
    load_sem, send_sem, recv_sem,
):
    me_r = lax.axis_index("row")
    me_c = lax.axis_index("col")
    size = {"row": nr, "col": nc}
    me_of = {"row": me_r, "col": me_c}

    def lanes(tile):
        return pl.ds(pl.multiple_of(tile * EDGE, EDGE), EDGE)

    def copy(x, axis, peer, src, dst):
        return pltpu.make_async_remote_copy(
            src_ref=src, dst_ref=dst,
            send_sem=send_sem.at[x, peer], recv_sem=recv_sem.at[x, me_of[axis]],
            device_id={axis: peer}, device_id_type=MESH,
        )

    def send_all(x, axis, src_of, dst):
        n, me = size[axis], me_of[axis]

        @pl.loop(1, n)
        def _(k):
            peer = lax.rem(me + k, n)
            copy(x, axis, peer, src_of(peer), dst).start()

    def wait_from(x, axis, source, ref):
        pltpu.make_async_remote_copy(
            src_ref=ref, dst_ref=ref,
            send_sem=send_sem.at[x, source], recv_sem=recv_sem.at[x, source],
            device_id={axis: source}, device_id_type=MESH,
        ).wait_recv()

    def wait_all(x, axis, dst_of):
        n, me = size[axis], me_of[axis]

        @pl.loop(1, n)
        def _(k):
            source = lax.rem(me + k, n)
            wait_from(x, axis, source, dst_of(source))

    def drain(x, axis, ref):
        n, me = size[axis], me_of[axis]

        @pl.loop(1, n)
        def _(k):
            peer = lax.rem(me + k, n)
            copy(x, axis, peer, ref, ref).wait_send()

    load = pltpu.make_async_copy(tiles_hbm, tiles.at[pl.ds(0, slots)], load_sem)
    load.start()
    barrier = pltpu.get_barrier_semaphore()
    for axis in ("row", "col"):
        @pl.loop(1, size[axis])
        def _(k):
            peer = lax.rem(me_of[axis] + k, size[axis])
            pl.semaphore_signal(barrier, inc=1, device_id={axis: peer}, device_id_type=MESH)
    own_s[...] = start_ref[...].astype(F32).T.astype(BF16)
    sT[:, lanes(me_c)] = own_s[...]
    tiles[slots] = jnp.zeros((EDGE, EDGE), BF16)
    pl.semaphore_wait(barrier, nr + nc - 2)

    send_all(0, "col", lambda peer: own_s, sT.at[:, lanes(me_c)])

    load.wait()

    def fold(s, total):
        return total + jnp.where(cell[s] == 0, tiles[s], jnp.zeros((EDGE, EDGE), BF16))

    corner = lax.fori_loop(0, slots, fold, jnp.zeros((EDGE, EDGE), BF16))

    @pl.loop(0, nc)
    def _(i):
        most = jnp.zeros((EDGE, EDGE), BF16)
        for j in range(nr):
            tile = tiles[table[i * nr + j]]
            if j == 0:
                tile = jnp.where(i == 0, corner, tile)
            dense[lanes(i), j * EDGE:(j + 1) * EDGE] = tile
            most = jnp.maximum(most, jnp.abs(tile))
        rbuf[me_c, pl.ds(i, 1), :] = jnp.max(most.astype(F32).T, axis=0, keepdims=True)

    send_all(1, "col", lambda peer: rbuf.at[me_c], rbuf.at[me_c])

    @pl.loop(0, nr)
    def _(j):
        most = jnp.zeros((EDGE, EDGE), BF16)
        for i in range(nc):
            most = jnp.maximum(most, jnp.abs(dense[i * EDGE:(i + 1) * EDGE, lanes(j)]))
        cbuf[me_r, pl.ds(j, 1), :] = jnp.max(most.astype(F32), axis=0, keepdims=True)

    send_all(2, "row", lambda peer: cbuf.at[me_r], cbuf.at[me_r])
    wait_all(1, "col", lambda source: rbuf.at[source])
    scale_r[...] = 1.0 / jnp.sqrt(jnp.max(rbuf[...], axis=0))
    wait_all(0, "col", lambda source: sT.at[:, lanes(source)])

    for t in range(nc):
        here = slice(t * EDGE, (t + 1) * EDGE)
        w1[:, here] = (scale_r[t:t + 1, :] * sT[:, here].astype(F32)).astype(BF16)

    def product(x, which, axis, w):
        n, me = size[axis], me_of[axis]
        half = n // 2
        part, land = parts.at[which], lands.at[which]

        @pl.loop(0, half)
        def _(q):
            pair = lax.rem(me // 2 + 1 + q, half)
            wide = pl.ds(pl.multiple_of(pair * 2 * EDGE, 2 * EDGE), 2 * EDGE)
            if axis == "row":
                y = jnp.dot(w[...], dense[:, wide], preferred_element_type=F32)
            else:
                y = lax.dot_general(
                    w[...], dense[wide, :], (((1,), (1,)), ((), ())), preferred_element_type=F32
                )
            for h in range(2):
                peer = pair * 2 + h
                part[peer] = y[:, h * EDGE:(h + 1) * EDGE]

                @pl.when(peer != me)
                def _():
                    copy(x, axis, peer, part.at[peer], land.at[me]).start()

        def add(k, total):
            source = lax.rem(me + k, n)
            wait_from(x, axis, source, land.at[source])
            return total + land[source]

        return lax.fori_loop(1, n, add, part[me])

    def spread(x, axis, tile, w):
        slot = 0 if w is w2 else (1 if w is w3 else 2)
        me = me_of[axis]
        own_w[slot] = tile
        send_all(x, axis, lambda peer: own_w.at[slot], w.at[:, lanes(me)])
        w[:, lanes(me)] = tile
        wait_all(x, axis, lambda source: w.at[:, lanes(source)])

    share = EDGE // nc

    def eighth(p):
        return pl.ds(pl.multiple_of(p * share, share), share)

    def gram_sum(x, which, local):
        part, a, s, b, full = gpart.at[which], ga.at[which], gs.at[which], gb.at[which], gfull.at[which]
        part[...] = local
        send_all(x, "col", lambda peer: part.at[eighth(peer)], a.at[me_c])
        a[me_c] = part[eighth(me_c), :]
        wait_all(x, "col", lambda source: a.at[source])
        mine = jnp.sum(a[...], axis=0)
        s[...] = mine
        send_all(x + 1, "row", lambda peer: s, b.at[me_r])
        b[me_r] = mine
        wait_all(x + 1, "row", lambda source: b.at[source])
        full[eighth(me_c), :] = jnp.sum(b[...], axis=0) / order
        send_all(x + 2, "col", lambda peer: full.at[eighth(me_c)], full.at[eighth(me_c)])
        wait_all(x + 2, "col", lambda source: full.at[eighth(source)])
        return full[...]

    def gram_drain(x, which):
        drain(x, "col", gpart.at[which, pl.ds(0, share)])
        drain(x + 1, "row", gs.at[which])
        drain(x + 2, "col", gpart.at[which, pl.ds(0, share)])

    p1 = product(3, 0, "row", w1)
    wait_all(2, "row", lambda source: cbuf.at[source])
    scale_c[...] = 1.0 / jnp.sqrt(jnp.max(cbuf[...], axis=0))
    mine_c = scale_c[pl.ds(me_r, 1), :]
    mine_r = scale_r[pl.ds(me_c, 1), :]
    spread(4, "row", (mine_c * mine_c * p1).astype(BF16), w2)
    p2 = product(5, 1, "col", w2)
    spread(6, "col", (mine_r * mine_r * p2).astype(BF16), w3)
    p3 = product(7, 2, "row", w3)
    iterate = mine_c * p3

    def outer(v):
        return lax.dot_general(
            v, v, (((1,), (1,)), ((), ())), precision=HIGH, preferred_element_type=F32
        )

    gram = gram_sum(8, 0, outer(iterate))

    elim[:, :EDGE] = gram
    row_id = lax.broadcasted_iota(jnp.int32, (EDGE, EDGE), 0)
    lane_id = lax.broadcasted_iota(jnp.int32, (EDGE, EDGE), 1)
    elim[:, EDGE:] = jnp.where(row_id == lane_id, 1.0, 0.0)
    lane = lax.broadcasted_iota(jnp.int32, (PANEL, EDGE), 1)
    sub = lax.broadcasted_iota(jnp.int32, (PANEL, EDGE), 0)

    @pl.loop(0, EDGE // PANEL)
    def _(p):
        rows = pl.ds(pl.multiple_of(p * PANEL, PANEL), PANEL)
        left = elim[rows, :EDGE]
        right = elim[rows, EDGE:]
        column = [
            jnp.broadcast_to(
                jnp.sum(jnp.where(lane == p * PANEL + k, left, 0.0), axis=1, keepdims=True),
                (PANEL, EDGE),
            )
            for k in range(PANEL)
        ]
        for k in range(PANEL):
            inv = 1.0 / jnp.sqrt(column[k][k:k + 1, :])
            step = jnp.where(sub > k, column[k] * inv, 0.0)
            l_row = left[k:k + 1, :] * inv
            r_row = right[k:k + 1, :] * inv
            left = jnp.where(sub == k, l_row, left - step * l_row)
            right = jnp.where(sub == k, r_row, right - step * r_row)
            for m in range(k + 1, PANEL):
                column[m] = column[m] - step * (column[m][k:k + 1, :] * inv)
        elim[rows, :EDGE] = left
        elim[rows, EDGE:] = right
        later = jnp.where(lane >= (p + 1) * PANEL, left, 0.0)
        whole = jnp.concatenate([left, right], axis=1)
        elim[...] -= lax.dot_general(
            later, whole, (((0,), (0,)), ((), ())), precision=HIGH, preferred_element_type=F32
        )

    basis = jnp.dot(elim[:, EDGE:], iterate, precision=HIGH, preferred_element_type=F32)
    spread(11, "row", (mine_c * basis).astype(BF16), w4)
    p4 = product(12, 3, "col", w4)
    ritz = mine_r * p4
    ritz_ref[...] = ritz.T
    gram_ref[...] = gram_sum(13, 1, outer(ritz))

    drain(0, "col", own_s)
    drain(1, "col", rbuf.at[me_c])
    drain(2, "row", cbuf.at[me_r])
    drain(3, "row", parts.at[0, 0])
    drain(4, "row", own_s)
    drain(5, "col", parts.at[0, 0])
    drain(6, "col", own_s)
    drain(7, "row", parts.at[0, 0])
    gram_drain(8, 0)
    drain(11, "row", own_s)
    drain(12, "col", parts.at[0, 0])
    gram_drain(13, 1)


def local(affinity_tiles, tile_index, start_block):
    nr, nc = lax.axis_size("row"), lax.axis_size("col")
    stored = affinity_tiles[0, 0]
    index = tile_index[0, 0]
    slots = stored.shape[0]
    cell = index[0] * nr + index[1]
    hit = cell[:, None] == jnp.arange(nr * nc, dtype=jnp.int32)[None, :]
    number = jnp.arange(slots, dtype=jnp.int32)[:, None]
    table = jnp.min(jnp.where(hit, number, slots), axis=0)
    most = max(nr, nc)
    share = EDGE // nc
    tile = (EDGE, EDGE)
    vmem = pltpu.VMEM
    return pl.pallas_call(
        functools.partial(kernel, nr, nc, slots, nr * nc * EDGE),
        out_shape=(jax.ShapeDtypeStruct(tile, F32), jax.ShapeDtypeStruct(tile, F32)),
        in_specs=[
            pl.BlockSpec(memory_space=pl.ANY),
            pl.BlockSpec(memory_space=pltpu.SMEM),
            pl.BlockSpec(memory_space=pltpu.SMEM),
            pl.BlockSpec(memory_space=pltpu.VMEM),
        ],
        out_specs=(pl.BlockSpec(memory_space=pltpu.VMEM), pl.BlockSpec(memory_space=pltpu.VMEM)),
        scratch_shapes=[
            vmem((slots + 1, *tile), BF16),
            vmem((nc * EDGE, nr * EDGE), BF16),
            vmem((nc, nc, EDGE), F32),
            vmem((nr, nr, EDGE), F32),
            vmem((nc, EDGE), F32),
            vmem((nr, EDGE), F32),
            vmem(tile, BF16),
            vmem((3, *tile), BF16),
            vmem((EDGE, nc * EDGE), BF16),
            vmem((EDGE, nc * EDGE), BF16),
            vmem((EDGE, nr * EDGE), BF16),
            vmem((EDGE, nc * EDGE), BF16),
            vmem((EDGE, nr * EDGE), BF16),
            vmem((4, most, *tile), F32),
            vmem((4, most, *tile), F32),
            vmem((2, *tile), F32),
            vmem((2, nc, share, EDGE), F32),
            vmem((2, share, EDGE), F32),
            vmem((2, nr, share, EDGE), F32),
            vmem((2, *tile), F32),
            vmem((EDGE, 2 * EDGE), F32),
            pltpu.SemaphoreType.DMA,
            pltpu.SemaphoreType.DMA((16, most)),
            pltpu.SemaphoreType.DMA((16, most)),
        ],
        compiler_params=pltpu.CompilerParams(
            collective_id=0, has_side_effects=True, vmem_limit_bytes=48 * 2**20
        ),
    )(stored, table, cell, start_block)


def solution(mesh):
    placed = (
        P("row", "col", None, None, None),
        P("row", "col", None, None),
        P(("row", "col"), None),
    )
    return jax.shard_map(
        local, mesh=mesh, in_specs=placed, out_specs=(P(("row", "col"), None), P()), check_vma=False
    )
```

```python
import functools

import jax
import jax.numpy as jnp
from jax import lax
from jax.experimental import pallas as pl
from jax.experimental.pallas import tpu as pltpu
from jax.sharding import PartitionSpec as P

EDGE = 128
PANEL = 16
CHAINS = 1
LAG_ROW = 8
LAG_COL = 2
NEAR = 4
FAR_FIRST = True
MESH = pl.DeviceIdType.MESH
HIGH = lax.Precision.HIGHEST
F32 = jnp.float32
BF16 = jnp.bfloat16


def kernel(
    nr, nc, slots, order,
    tiles_hbm, start_hbm, table, cell,
    ritz_ref, gram_ref,
    tiles, start, dense, rbuf, cbuf, scale_r, scale_c,
    sT, w1, w2, w3, w4, x4,
    kept, given, land1, land2, gpart, ga, gs, gb, gfull, elim,
    load_sem, send_sem, recv_sem,
):
    me_of = {"row": lax.axis_index("row"), "col": lax.axis_index("col")}
    me_r, me_c = me_of["row"], me_of["col"]
    size = {"row": nr, "col": nc}
    deep = EDGE // CHAINS
    pending = []

    def lanes(tile):
        return pl.ds(pl.multiple_of(tile * EDGE, EDGE), EDGE)

    def copy(x, axis, peer, src, dst, slot):
        return pltpu.make_async_remote_copy(
            src_ref=src, dst_ref=dst, send_sem=send_sem.at[x], recv_sem=recv_sem.at[x, slot],
            device_id={axis: peer}, device_id_type=MESH,
        )

    def arrived(x, axis, ref, slot):
        copy(x, axis, me_of[axis], ref, ref, slot).wait_recv()

    def sent(x, axis, ref):
        pending.append(lambda: copy(x, axis, me_of[axis], ref, ref, 0).wait_send())

    def flush():
        while pending:
            pending.pop(0)()

    def place(axis):
        me = me_of[axis]
        return size[axis] // 2, me // 2, lax.rem(me, 2), me + 1 - 2 * lax.rem(me, 2)

    def group_at(axis, k):
        groups, mine, _, _ = place(axis)
        return lax.rem(mine + groups // 2 + (k + 1) // 2 * (2 * lax.rem(k, 2) - 1) + groups, groups)

    def others(axis, body):
        @pl.loop(0, size[axis])
        def _(k):
            peer = group_at(axis, k // 2) * 2 + lax.rem(k, 2)

            @pl.when(peer != me_of[axis])
            def _():
                body(peer)

    def send_all(x, axis, src_of, dst):
        others(axis, lambda peer: copy(x, axis, peer, src_of(peer), dst, me_of[axis]).start())

    def wait_all(x, axis, dst_of):
        n, me = size[axis], me_of[axis]

        @pl.loop(1, n)
        def _(k):
            source = lax.rem(me + k, n)
            arrived(x, axis, dst_of(source), source)

    load = pltpu.make_async_copy(tiles_hbm, tiles.at[pl.ds(0, slots)], load_sem.at[0])
    load.start()
    load_start = pltpu.make_async_copy(start_hbm, start, load_sem.at[1])
    load_start.start()
    barrier = pltpu.get_barrier_semaphore()
    for axis in ("row", "col"):
        others(axis, lambda peer, axis=axis: pl.semaphore_signal(
            barrier, inc=1, device_id={axis: peer}, device_id_type=MESH
        ))

    def depth(s):
        return pl.ds(s * deep, deep)

    whole = pl.ds(0, EDGE)

    def gather_send(x, axis, rows, tile, w):
        groups, mine, side, partner = place(axis)
        here = w.at[rows, lanes(me_of[axis])]
        w[rows, lanes(me_of[axis])] = tile

        @pl.loop(0, groups - 1)
        def _(k):
            copy(x, axis, group_at(axis, order_of(k, groups)) * 2 + side, here, here, mine).start()

        copy(x, axis, partner, here, here, groups + mine).start()
        sent(x, axis, w.at[rows, pl.ds(0, groups * EDGE)])

    def gather_pass(x, axis, rows, w, begin=0, end=None):
        groups, mine, side, partner = place(axis)
        last = end is None

        @pl.loop(begin, groups - 1 if last else end)
        def _(k):
            g = group_at(axis, order_of(k, groups))
            here = w.at[rows, lanes(g * 2 + side)]
            arrived(x, axis, here, g)
            copy(x + 1, axis, partner, here, here, groups + g).start()

        if last:
            sent(x + 1, axis, w.at[rows, pl.ds(0, (groups - 1) * EDGE)])

    def order_of(k, groups):
        return k if FAR_FIRST else groups - 2 - k

    def gather_wait(x, axis, rows, w):
        groups, mine, side, partner = place(axis)
        arrived(x, axis, w.at[rows, lanes(partner)], groups + mine)

        @pl.loop(0, groups - 1)
        def _(k):
            g = group_at(axis, order_of(k, groups))
            arrived(x + 1, axis, w.at[rows, lanes(g * 2 + 1 - side)], groups + g)

    def product(x, axis, rows, which, w, lag, between=None):
        groups, mine, side, partner = place(axis)
        keep, give, land = kept.at[which], given.at[which], land1.at[which]

        def multiply(k):
            g = group_at(axis, k)
            wide = pl.ds(pl.multiple_of(g * 2 * EDGE, 2 * EDGE), 2 * EDGE)
            if axis == "row":
                y = jnp.dot(w[rows, :], dense[:, wide], preferred_element_type=F32)
            else:
                y = lax.dot_general(
                    w[rows, :], dense[wide, :], (((1,), (1,)), ((), ())),
                    preferred_element_type=F32,
                )
            first, second = y[:, :EDGE], y[:, EDGE:]
            keep[g, rows, :] = jnp.where(side == 0, first, second)
            give[g, rows, :] = jnp.where(side == 0, second, first)
            copy(x, axis, partner, give.at[g, rows, :], land.at[g, rows, :], g).start()

        lag = lag * groups // 8

        @pl.loop(0, groups)
        def _(k):
            multiply(k)
            if lag < groups:
                @pl.when(k >= lag)
                def _():
                    pair_sum(x, axis, rows, which, k - lag)

        if between:
            between()

        @pl.loop(groups - lag, groups)
        def _(k):
            pair_sum(x, axis, rows, which, k)

        sent(x, axis, give.at[:, rows, :])
        sent(x + 1, axis, keep.at[pl.ds(0, groups - 1), rows, :])

    def pair_sum(x, axis, rows, which, k):
        groups, mine, side, partner = place(axis)
        keep, land = kept.at[which], land1.at[which]
        g = group_at(axis, k)
        arrived(x, axis, land.at[g, rows, :], g)
        keep[g, rows, :] = keep[g, rows, :] + land[g, rows, :]

        @pl.when(k < groups - 1)
        def _():
            copy(
                x + 1, axis, g * 2 + side, keep.at[g, rows, :], land2.at[which, mine, rows, :], mine
            ).start()

    def total_sum(x, axis, rows, which):
        groups, mine, side, partner = place(axis)
        land = land2.at[which]

        def add(k, total):
            g = group_at(axis, groups - 2 - k)
            arrived(x + 1, axis, land.at[g, rows, :], g)
            return total + land[g, rows, :]

        return lax.fori_loop(0, groups - 1, add, kept[which, mine, rows, :])

    chains = [depth(s) for s in range(CHAINS)]
    lag = {"row": LAG_ROW, "col": LAG_COL}

    tiles[slots] = jnp.zeros((EDGE, EDGE), BF16)
    load_start.wait()
    sT[:, lanes(me_c)] = start[...].astype(F32).T.astype(BF16)
    load.wait()

    def fold(s, total):
        return total + jnp.where(cell[s] == 0, tiles[s], jnp.zeros((EDGE, EDGE), BF16))

    tiles[slots + 1] = lax.fori_loop(0, slots, fold, jnp.zeros((EDGE, EDGE), BF16))

    @pl.loop(0, nc)
    def _(i):
        most = jnp.zeros((EDGE, EDGE), BF16)
        for j in range(nr):
            which = table[i * nr + j]
            if j == 0:
                which = jnp.where(i == 0, slots + 1, which)
            tile = tiles[which]
            dense[lanes(i), j * EDGE:(j + 1) * EDGE] = tile
            most = jnp.maximum(most, jnp.abs(tile))
        rbuf[me_c, pl.ds(i, 1), :] = jnp.max(most.astype(F32).T, axis=0, keepdims=True)

    pl.semaphore_wait(barrier, nr + nc - 2)
    gather_send(0, "col", whole, sT[:, lanes(me_c)], sT)
    send_all(2, "col", lambda peer: rbuf.at[me_c], rbuf.at[me_c])
    sent(2, "col", rbuf.at[pl.ds(0, nc - 1)])

    @pl.loop(0, nr)
    def _(j):
        most = jnp.zeros((EDGE, EDGE), BF16)
        for i in range(nc):
            most = jnp.maximum(most, jnp.abs(dense[i * EDGE:(i + 1) * EDGE, lanes(j)]))
        cbuf[me_r, pl.ds(j, 1), :] = jnp.max(most.astype(F32), axis=0, keepdims=True)

    gather_pass(0, "col", whole, sT)
    wait_all(2, "col", lambda source: rbuf.at[source])
    scale_r[...] = 1.0 / jnp.sqrt(jnp.max(rbuf[...], axis=0))
    mine_r = scale_r[pl.ds(me_c, 1), :]
    gather_wait(0, "col", whole, sT)
    for t in range(nc):
        here = slice(t * EDGE, (t + 1) * EDGE)
        w1[:, here] = (scale_r[t:t + 1, :] * sT[:, here].astype(F32)).astype(BF16)
    x = 4

    def after_product():
        send_all(3, "row", lambda peer: cbuf.at[me_r], cbuf.at[me_r])
        sent(3, "row", cbuf.at[pl.ds(0, nr - 1)])

    for s, rows in enumerate(chains):
        product(x + 2 * s, "row", rows, 0, w1, lag["row"], after_product if s == 0 else None)
    flush()
    wait_all(3, "row", lambda source: cbuf.at[source])
    scale_c[...] = 1.0 / jnp.sqrt(jnp.max(cbuf[...], axis=0))
    mine_c = scale_c[pl.ds(me_r, 1), :]

    def turn(x, axis, which, scale, w, other):
        y = x + 2 * CHAINS
        for s, rows in enumerate(chains):
            tile = (scale * scale * total_sum(x + 2 * s, axis, rows, which)).astype(BF16)
            gather_send(y + 2 * s, axis, rows, tile, w)
        for s, rows in enumerate(chains):
            gather_pass(y + 2 * s, axis, rows, w)
        z = y + 2 * CHAINS
        for s, rows in enumerate(chains):
            gather_wait(y + 2 * s, axis, rows, w)
            product(z + 2 * s, other, rows, which + 1, w, lag[other])
        flush()
        return z

    x = turn(x, "row", 0, mine_c, w2, "col")
    x = turn(x, "col", 1, mine_r, w3, "row")
    iterate = mine_c * jnp.concatenate(
        [total_sum(x + 2 * s, "row", rows, 2) for s, rows in enumerate(chains)], axis=0
    )
    x += 2 * CHAINS

    def outer(v):
        return lax.dot_general(
            v, v, (((1,), (1,)), ((), ())), precision=HIGH, preferred_element_type=F32
        )

    share = EDGE // nc

    def strip(p):
        return pl.ds(pl.multiple_of(p * share, share), share)

    def gram_sum(x, which, local, first=None, second=None, third=None):
        part, a, s, b, full = gpart.at[which], ga.at[which], gs.at[which], gb.at[which], gfull.at[which]
        part[...] = local
        send_all(x, "col", lambda peer: part.at[strip(peer)], a.at[me_c])
        sent(x, "col", a.at[pl.ds(0, nc - 1)])
        a[me_c] = part[strip(me_c), :]
        if first:
            first()
        wait_all(x, "col", lambda source: a.at[source])
        mine = jnp.sum(a[...], axis=0)
        s[...] = mine
        send_all(x + 1, "row", lambda peer: s, b.at[me_r])
        sent(x + 1, "row", b.at[pl.ds(0, nr - 1)])
        b[me_r] = mine
        if second:
            second()
        wait_all(x + 1, "row", lambda source: b.at[source])
        full[strip(me_c), :] = jnp.sum(b[...], axis=0) / order
        send_all(x + 2, "col", lambda peer: full.at[strip(me_c)], full.at[strip(me_c)])
        sent(x + 2, "col", a.at[pl.ds(0, nc - 1)])
        if third:
            third()
        wait_all(x + 2, "col", lambda source: full.at[strip(source)])
        return full[...]

    near = NEAR * nr // 16
    gram = gram_sum(
        x, 0, outer(iterate),
        lambda: gather_send(x + 3, "row", whole, iterate, x4),
        lambda: gather_pass(x + 3, "row", whole, x4, 0, near),
        lambda: gather_pass(x + 3, "row", whole, x4, near),
    )
    flush()

    elim[:, :EDGE] = gram
    row_id = lax.broadcasted_iota(jnp.int32, (EDGE, EDGE), 0)
    lane_id = lax.broadcasted_iota(jnp.int32, (EDGE, EDGE), 1)
    elim[:, EDGE:] = jnp.where(row_id == lane_id, 1.0, 0.0)
    lane = lax.broadcasted_iota(jnp.int32, (PANEL, EDGE), 1)
    sub = lax.broadcasted_iota(jnp.int32, (PANEL, EDGE), 0)

    @pl.loop(0, EDGE // PANEL)
    def _(p):
        rows = pl.ds(pl.multiple_of(p * PANEL, PANEL), PANEL)
        left = elim[rows, :EDGE]
        right = elim[rows, EDGE:]
        column = [
            jnp.broadcast_to(
                jnp.sum(jnp.where(lane == p * PANEL + k, left, 0.0), axis=1, keepdims=True),
                (PANEL, EDGE),
            )
            for k in range(PANEL)
        ]
        for k in range(PANEL):
            inv = 1.0 / jnp.sqrt(column[k][k:k + 1, :])
            step = jnp.where(sub > k, column[k] * inv, 0.0)
            l_row = left[k:k + 1, :] * inv
            r_row = right[k:k + 1, :] * inv
            left = jnp.where(sub == k, l_row, left - step * l_row)
            right = jnp.where(sub == k, r_row, right - step * r_row)
            for m in range(k + 1, PANEL):
                column[m] = column[m] - step * (column[m][k:k + 1, :] * inv)
        elim[rows, :EDGE] = left
        elim[rows, EDGE:] = right
        later = jnp.where(lane >= (p + 1) * PANEL, left, 0.0)
        both = jnp.concatenate([left, right], axis=1)
        elim[...] -= lax.dot_general(
            later, both, (((0,), (0,)), ((), ())), precision=HIGH, preferred_element_type=F32
        )

    gather_wait(x + 3, "row", whole, x4)
    inverse = elim[:, EDGE:]
    for t in range(0, nr, 2):
        here = slice(t * EDGE, (t + 2) * EDGE)
        basis = jnp.dot(inverse, x4[:, here], precision=HIGH, preferred_element_type=F32)
        both = jnp.concatenate([scale_c[t:t + 1, :], scale_c[t + 1:t + 2, :]], axis=1)
        w4[:, here] = (both * basis).astype(BF16)
    x += 5
    product(x, "col", whole, 3, w4, lag["col"])
    ritz = mine_r * total_sum(x, "col", whole, 3)
    x += 2
    ritz_ref[...] = ritz.T
    gram_ref[...] = gram_sum(x, 1, outer(ritz), flush)
    flush()


def local(affinity_tiles, tile_index, start_block):
    nr, nc = lax.axis_size("row"), lax.axis_size("col")
    stored = affinity_tiles[0, 0]
    index = tile_index[0, 0]
    slots = stored.shape[0]
    cell = index[0] * nr + index[1]
    hit = cell[:, None] == jnp.arange(nr * nc, dtype=jnp.int32)[None, :]
    number = jnp.arange(slots, dtype=jnp.int32)[:, None]
    table = jnp.min(jnp.where(hit, number, slots), axis=0)
    most = max(nr, nc)
    groups = most // 2
    share = EDGE // nc
    tile = (EDGE, EDGE)
    exchanges = 14 + 10 * CHAINS
    vmem = pltpu.VMEM
    return pl.pallas_call(
        functools.partial(kernel, nr, nc, slots, nr * nc * EDGE),
        out_shape=(jax.ShapeDtypeStruct(tile, F32), jax.ShapeDtypeStruct(tile, F32)),
        in_specs=[
            pl.BlockSpec(memory_space=pl.ANY),
            pl.BlockSpec(memory_space=pl.ANY),
            pl.BlockSpec(memory_space=pltpu.SMEM),
            pl.BlockSpec(memory_space=pltpu.SMEM),
        ],
        out_specs=(pl.BlockSpec(memory_space=pltpu.VMEM), pl.BlockSpec(memory_space=pltpu.VMEM)),
        scratch_shapes=[
            vmem((slots + 2, *tile), BF16),
            vmem(tile, BF16),
            vmem((nc * EDGE, nr * EDGE), BF16),
            vmem((nc, nc, EDGE), F32),
            vmem((nr, nr, EDGE), F32),
            vmem((nc, EDGE), F32),
            vmem((nr, EDGE), F32),
            vmem((EDGE, nc * EDGE), BF16),
            vmem((EDGE, nc * EDGE), BF16),
            vmem((EDGE, nr * EDGE), BF16),
            vmem((EDGE, nc * EDGE), BF16),
            vmem((EDGE, nr * EDGE), BF16),
            vmem((EDGE, nr * EDGE), F32),
            vmem((4, groups, *tile), F32),
            vmem((4, groups, *tile), F32),
            vmem((4, groups, *tile), F32),
            vmem((4, groups, *tile), F32),
            vmem((2, *tile), F32),
            vmem((2, nc, share, EDGE), F32),
            vmem((2, share, EDGE), F32),
            vmem((2, nr, share, EDGE), F32),
            vmem((2, *tile), F32),
            vmem((EDGE, 2 * EDGE), F32),
            pltpu.SemaphoreType.DMA((2,)),
            pltpu.SemaphoreType.DMA((exchanges,)),
            pltpu.SemaphoreType.DMA((exchanges, most)),
        ],
        compiler_params=pltpu.CompilerParams(
            collective_id=0, has_side_effects=True, vmem_limit_bytes=48 * 2**20
        ),
    )(stored, start_block, table, cell)


def solution(mesh):
    placed = (
        P("row", "col", None, None, None),
        P("row", "col", None, None),
        P(("row", "col"), None),
    )
    return jax.shard_map(
        local, mesh=mesh, in_specs=placed, out_specs=(P(("row", "col"), None), P()), check_vma=False
    )
```

```python
import functools

import jax
import jax.numpy as jnp
from jax import lax
from jax.experimental import pallas as pl
from jax.experimental.pallas import tpu as pltpu
from jax.sharding import PartitionSpec as P

EDGE = 128
PANEL = 16
CHAINS = 1
LAG_ROW = 8
LAG_COL = 2
NEAR = 4
FAR_FIRST = True
MESH = pl.DeviceIdType.MESH
HIGH = lax.Precision.HIGHEST
F32 = jnp.float32
BF16 = jnp.bfloat16


def kernel(
    nr, nc, slots, order,
    tiles_hbm, start_hbm, table, cell,
    ritz_ref, gram_ref,
    tiles, start, dense, rbuf, cbuf, scale_r, scale_c,
    sT, w1, w2, w3, w4, x4,
    kept, given, land1, land2, gpart, ga, gs, gb, gfull, elim,
    load_sem, send_sem, recv_sem,
):
    me_of = {"row": lax.axis_index("row"), "col": lax.axis_index("col")}
    me_r, me_c = me_of["row"], me_of["col"]
    size = {"row": nr, "col": nc}
    deep = EDGE // CHAINS
    pending = []

    def lanes(tile):
        return pl.ds(pl.multiple_of(tile * EDGE, EDGE), EDGE)

    def copy(x, axis, peer, src, dst, slot):
        return pltpu.make_async_remote_copy(
            src_ref=src, dst_ref=dst, send_sem=send_sem.at[x], recv_sem=recv_sem.at[x, slot],
            device_id={axis: peer}, device_id_type=MESH,
        )

    def arrived(x, axis, ref, slot):
        copy(x, axis, me_of[axis], ref, ref, slot).wait_recv()

    def sent(x, axis, ref):
        pending.append(lambda: copy(x, axis, me_of[axis], ref, ref, 0).wait_send())

    def flush():
        while pending:
            pending.pop(0)()

    def place(axis):
        me = me_of[axis]
        return size[axis] // 2, me // 2, lax.rem(me, 2), me + 1 - 2 * lax.rem(me, 2)

    def group_at(axis, k):
        groups, mine, _, _ = place(axis)
        return lax.rem(mine + groups // 2 + (k + 1) // 2 * (2 * lax.rem(k, 2) - 1) + groups, groups)

    def others(axis, body):
        @pl.loop(0, size[axis])
        def _(k):
            peer = group_at(axis, k // 2) * 2 + lax.rem(k, 2)

            @pl.when(peer != me_of[axis])
            def _():
                body(peer)

    def send_all(x, axis, src_of, dst):
        others(axis, lambda peer: copy(x, axis, peer, src_of(peer), dst, me_of[axis]).start())

    def wait_all(x, axis, dst_of):
        n, me = size[axis], me_of[axis]

        @pl.loop(1, n)
        def _(k):
            source = lax.rem(me + k, n)
            arrived(x, axis, dst_of(source), source)

    load = pltpu.make_async_copy(tiles_hbm, tiles.at[pl.ds(0, slots)], load_sem.at[0])
    load.start()
    load_start = pltpu.make_async_copy(start_hbm, start, load_sem.at[1])
    load_start.start()
    barrier = pltpu.get_barrier_semaphore()
    for axis in ("row", "col"):
        others(axis, lambda peer, axis=axis: pl.semaphore_signal(
            barrier, inc=1, device_id={axis: peer}, device_id_type=MESH
        ))

    def depth(s):
        return pl.ds(s * deep, deep)

    whole = pl.ds(0, EDGE)

    def gather_send(x, axis, rows, tile, w):
        groups, mine, side, partner = place(axis)
        here = w.at[rows, lanes(me_of[axis])]
        w[rows, lanes(me_of[axis])] = tile

        @pl.loop(0, groups - 1)
        def _(k):
            copy(x, axis, group_at(axis, order_of(k, groups)) * 2 + side, here, here, mine).start()

        copy(x, axis, partner, here, here, groups + mine).start()
        sent(x, axis, w.at[rows, pl.ds(0, groups * EDGE)])

    def gather_pass(x, axis, rows, w, begin=0, end=None):
        groups, mine, side, partner = place(axis)
        last = end is None

        @pl.loop(begin, groups - 1 if last else end)
        def _(k):
            g = group_at(axis, order_of(k, groups))
            here = w.at[rows, lanes(g * 2 + side)]
            arrived(x, axis, here, g)
            copy(x + 1, axis, partner, here, here, groups + g).start()

        if last:
            sent(x + 1, axis, w.at[rows, pl.ds(0, (groups - 1) * EDGE)])

    def order_of(k, groups):
        return k if FAR_FIRST else groups - 2 - k

    def gather_wait(x, axis, rows, w):
        groups, mine, side, partner = place(axis)
        arrived(x, axis, w.at[rows, lanes(partner)], groups + mine)

        @pl.loop(0, groups - 1)
        def _(k):
            g = group_at(axis, order_of(k, groups))
            arrived(x + 1, axis, w.at[rows, lanes(g * 2 + 1 - side)], groups + g)

    def product(x, axis, rows, which, w, lag, between=None):
        groups, mine, side, partner = place(axis)
        keep, give, land = kept.at[which], given.at[which], land1.at[which]

        def multiply(k):
            g = group_at(axis, k)
            wide = pl.ds(pl.multiple_of(g * 2 * EDGE, 2 * EDGE), 2 * EDGE)
            if axis == "row":
                y = jnp.dot(w[rows, :], dense[:, wide], preferred_element_type=F32)
            else:
                y = lax.dot_general(
                    w[rows, :], dense[wide, :], (((1,), (1,)), ((), ())),
                    preferred_element_type=F32,
                )
            first, second = y[:, :EDGE], y[:, EDGE:]
            keep[g, rows, :] = jnp.where(side == 0, first, second)
            give[g, rows, :] = jnp.where(side == 0, second, first)
            copy(x, axis, partner, give.at[g, rows, :], land.at[g, rows, :], g).start()

        lag = lag * groups // 8

        @pl.loop(0, groups)
        def _(k):
            multiply(k)
            if lag < groups:
                @pl.when(k >= lag)
                def _():
                    pair_sum(x, axis, rows, which, k - lag)

        if between:
            between()

        @pl.loop(groups - lag, groups)
        def _(k):
            pair_sum(x, axis, rows, which, k)

        sent(x, axis, give.at[:, rows, :])
        sent(x + 1, axis, keep.at[pl.ds(0, groups - 1), rows, :])

    def pair_sum(x, axis, rows, which, k):
        groups, mine, side, partner = place(axis)
        keep, land = kept.at[which], land1.at[which]
        g = group_at(axis, k)
        arrived(x, axis, land.at[g, rows, :], g)
        keep[g, rows, :] = keep[g, rows, :] + land[g, rows, :]

        @pl.when(k < groups - 1)
        def _():
            copy(
                x + 1, axis, g * 2 + side, keep.at[g, rows, :], land2.at[which, mine, rows, :], mine
            ).start()

    def total_sum(x, axis, rows, which):
        groups, mine, side, partner = place(axis)
        land = land2.at[which]

        def add(k, total):
            g = group_at(axis, groups - 2 - k)
            arrived(x + 1, axis, land.at[g, rows, :], g)
            return total + land[g, rows, :]

        return lax.fori_loop(0, groups - 1, add, kept[which, mine, rows, :])

    chains = [depth(s) for s in range(CHAINS)]
    lag = {"row": LAG_ROW, "col": LAG_COL}

    tiles[slots] = jnp.zeros((EDGE, EDGE), BF16)
    load_start.wait()
    sT[:, lanes(me_c)] = start[...].astype(F32).T.astype(BF16)
    load.wait()

    def fold(s, total):
        return total + jnp.where(cell[s] == 0, tiles[s], jnp.zeros((EDGE, EDGE), BF16))

    tiles[slots + 1] = lax.fori_loop(0, slots, fold, jnp.zeros((EDGE, EDGE), BF16), unroll=8)

    @pl.loop(0, nc)
    def _(i):
        most = jnp.zeros((EDGE, EDGE), BF16)
        for j in range(nr):
            which = table[i * nr + j]
            if j == 0:
                which = jnp.where(i == 0, slots + 1, which)
            tile = tiles[which]
            most = jnp.maximum(most, jnp.abs(tile))
        rbuf[me_c, pl.ds(i, 1), :] = jnp.max(most.astype(F32).T, axis=0, keepdims=True)

    pl.semaphore_wait(barrier, nr + nc - 2)
    gather_send(0, "col", whole, sT[:, lanes(me_c)], sT)
    send_all(2, "col", lambda peer: rbuf.at[me_c], rbuf.at[me_c])
    sent(2, "col", rbuf.at[pl.ds(0, nc - 1)])

    @pl.loop(0, nr)
    def _(j):
        most = jnp.zeros((EDGE, EDGE), BF16)
        for i in range(nc):
            which = table[i * nr + j]
            if i == 0:
                which = jnp.where(j == 0, slots + 1, which)
            tile = tiles[which]
            dense[i * EDGE:(i + 1) * EDGE, lanes(j)] = tile
            most = jnp.maximum(most, jnp.abs(tile))
        cbuf[me_r, pl.ds(j, 1), :] = jnp.max(most.astype(F32), axis=0, keepdims=True)

    send_all(3, "row", lambda peer: cbuf.at[me_r], cbuf.at[me_r])
    sent(3, "row", cbuf.at[pl.ds(0, nr - 1)])
    gather_pass(0, "col", whole, sT)
    wait_all(2, "col", lambda source: rbuf.at[source])
    scale_r[...] = 1.0 / jnp.sqrt(jnp.max(rbuf[...], axis=0))
    mine_r = scale_r[pl.ds(me_c, 1), :]
    gather_wait(0, "col", whole, sT)
    for t in range(nc):
        here = slice(t * EDGE, (t + 1) * EDGE)
        w1[:, here] = (scale_r[t:t + 1, :] * sT[:, here].astype(F32)).astype(BF16)
    x = 4

    for s, rows in enumerate(chains):
        product(x + 2 * s, "row", rows, 0, w1, lag["row"])
    flush()
    wait_all(3, "row", lambda source: cbuf.at[source])
    scale_c[...] = 1.0 / jnp.sqrt(jnp.max(cbuf[...], axis=0))
    mine_c = scale_c[pl.ds(me_r, 1), :]

    def turn(x, axis, which, scale, w, other):
        y = x + 2 * CHAINS
        for s, rows in enumerate(chains):
            tile = (scale * scale * total_sum(x + 2 * s, axis, rows, which)).astype(BF16)
            gather_send(y + 2 * s, axis, rows, tile, w)
        for s, rows in enumerate(chains):
            gather_pass(y + 2 * s, axis, rows, w)
        z = y + 2 * CHAINS
        for s, rows in enumerate(chains):
            gather_wait(y + 2 * s, axis, rows, w)
            product(z + 2 * s, other, rows, which + 1, w, lag[other])
        flush()
        return z

    x = turn(x, "row", 0, mine_c, w2, "col")
    x = turn(x, "col", 1, mine_r, w3, "row")
    iterate = mine_c * jnp.concatenate(
        [total_sum(x + 2 * s, "row", rows, 2) for s, rows in enumerate(chains)], axis=0
    )
    x += 2 * CHAINS

    def outer(v):
        return lax.dot_general(
            v, v, (((1,), (1,)), ((), ())), precision=HIGH, preferred_element_type=F32
        )

    share = EDGE // nc

    def strip(p):
        return pl.ds(pl.multiple_of(p * share, share), share)

    def gram_sum(x, which, local, first=None, second=None, third=None):
        part, a, s, b, full = gpart.at[which], ga.at[which], gs.at[which], gb.at[which], gfull.at[which]
        part[...] = local
        send_all(x, "col", lambda peer: part.at[strip(peer)], a.at[me_c])
        sent(x, "col", a.at[pl.ds(0, nc - 1)])
        a[me_c] = part[strip(me_c), :]
        if first:
            first()
        wait_all(x, "col", lambda source: a.at[source])
        mine = jnp.sum(a[...], axis=0)
        s[...] = mine
        send_all(x + 1, "row", lambda peer: s, b.at[me_r])
        sent(x + 1, "row", b.at[pl.ds(0, nr - 1)])
        b[me_r] = mine
        if second:
            second()
        wait_all(x + 1, "row", lambda source: b.at[source])
        full[strip(me_c), :] = jnp.sum(b[...], axis=0) / order
        send_all(x + 2, "col", lambda peer: full.at[strip(me_c)], full.at[strip(me_c)])
        sent(x + 2, "col", a.at[pl.ds(0, nc - 1)])
        if third:
            third()
        wait_all(x + 2, "col", lambda source: full.at[strip(source)])
        return full[...]

    near = NEAR * nr // 16
    gram = gram_sum(
        x, 0, outer(iterate),
        lambda: gather_send(x + 3, "row", whole, iterate, x4),
        lambda: gather_pass(x + 3, "row", whole, x4, 0, near),
        lambda: gather_pass(x + 3, "row", whole, x4, near),
    )
    flush()

    elim[:, :EDGE] = gram
    row_id = lax.broadcasted_iota(jnp.int32, (EDGE, EDGE), 0)
    lane_id = lax.broadcasted_iota(jnp.int32, (EDGE, EDGE), 1)
    elim[:, EDGE:] = jnp.where(row_id == lane_id, 1.0, 0.0)
    lane = lax.broadcasted_iota(jnp.int32, (PANEL, EDGE), 1)
    sub = lax.broadcasted_iota(jnp.int32, (PANEL, EDGE), 0)

    @pl.loop(0, EDGE // PANEL)
    def _(p):
        rows = pl.ds(pl.multiple_of(p * PANEL, PANEL), PANEL)
        left = elim[rows, :EDGE]
        right = elim[rows, EDGE:]
        column = [
            jnp.broadcast_to(
                jnp.sum(jnp.where(lane == p * PANEL + k, left, 0.0), axis=1, keepdims=True),
                (PANEL, EDGE),
            )
            for k in range(PANEL)
        ]
        for k in range(PANEL):
            inv = 1.0 / jnp.sqrt(column[k][k:k + 1, :])
            step = jnp.where(sub > k, column[k] * inv, 0.0)
            l_row = left[k:k + 1, :] * inv
            r_row = right[k:k + 1, :] * inv
            left = jnp.where(sub == k, l_row, left - step * l_row)
            right = jnp.where(sub == k, r_row, right - step * r_row)
            for m in range(k + 1, PANEL):
                column[m] = column[m] - step * (column[m][k:k + 1, :] * inv)
        elim[rows, :EDGE] = left
        elim[rows, EDGE:] = right
        later = jnp.where(lane >= (p + 1) * PANEL, left, 0.0)
        both = jnp.concatenate([left, right], axis=1)
        elim[...] -= lax.dot_general(
            later, both, (((0,), (0,)), ((), ())), precision=HIGH, preferred_element_type=F32
        )

    gather_wait(x + 3, "row", whole, x4)
    inverse = elim[:, EDGE:]
    for t in range(0, nr, 2):
        here = slice(t * EDGE, (t + 2) * EDGE)
        basis = jnp.dot(inverse, x4[:, here], precision=HIGH, preferred_element_type=F32)
        both = jnp.concatenate([scale_c[t:t + 1, :], scale_c[t + 1:t + 2, :]], axis=1)
        w4[:, here] = (both * basis).astype(BF16)
    x += 5
    product(x, "col", whole, 3, w4, lag["col"])
    ritz = mine_r * total_sum(x, "col", whole, 3)
    x += 2
    ritz_ref[...] = ritz.T
    gram_ref[...] = gram_sum(x, 1, outer(ritz), flush)
    flush()


def local(affinity_tiles, tile_index, start_block):
    nr, nc = lax.axis_size("row"), lax.axis_size("col")
    stored = affinity_tiles[0, 0]
    index = tile_index[0, 0]
    slots = stored.shape[0]
    cell = index[0] * nr + index[1]
    hit = cell[:, None] == jnp.arange(nr * nc, dtype=jnp.int32)[None, :]
    number = jnp.arange(slots, dtype=jnp.int32)[:, None]
    table = jnp.min(jnp.where(hit, number, slots), axis=0)
    most = max(nr, nc)
    groups = most // 2
    share = EDGE // nc
    tile = (EDGE, EDGE)
    exchanges = 14 + 10 * CHAINS
    vmem = pltpu.VMEM
    return pl.pallas_call(
        functools.partial(kernel, nr, nc, slots, nr * nc * EDGE),
        out_shape=(jax.ShapeDtypeStruct(tile, F32), jax.ShapeDtypeStruct(tile, F32)),
        in_specs=[
            pl.BlockSpec(memory_space=pl.ANY),
            pl.BlockSpec(memory_space=pl.ANY),
            pl.BlockSpec(memory_space=pltpu.SMEM),
            pl.BlockSpec(memory_space=pltpu.SMEM),
        ],
        out_specs=(pl.BlockSpec(memory_space=pltpu.VMEM), pl.BlockSpec(memory_space=pltpu.VMEM)),
        scratch_shapes=[
            vmem((slots + 2, *tile), BF16),
            vmem(tile, BF16),
            vmem((nc * EDGE, nr * EDGE), BF16),
            vmem((nc, nc, EDGE), F32),
            vmem((nr, nr, EDGE), F32),
            vmem((nc, EDGE), F32),
            vmem((nr, EDGE), F32),
            vmem((EDGE, nc * EDGE), BF16),
            vmem((EDGE, nc * EDGE), BF16),
            vmem((EDGE, nr * EDGE), BF16),
            vmem((EDGE, nc * EDGE), BF16),
            vmem((EDGE, nr * EDGE), BF16),
            vmem((EDGE, nr * EDGE), F32),
            vmem((4, groups, *tile), F32),
            vmem((4, groups, *tile), F32),
            vmem((4, groups, *tile), F32),
            vmem((4, groups, *tile), F32),
            vmem((2, *tile), F32),
            vmem((2, nc, share, EDGE), F32),
            vmem((2, share, EDGE), F32),
            vmem((2, nr, share, EDGE), F32),
            vmem((2, *tile), F32),
            vmem((EDGE, 2 * EDGE), F32),
            pltpu.SemaphoreType.DMA((2,)),
            pltpu.SemaphoreType.DMA((exchanges,)),
            pltpu.SemaphoreType.DMA((exchanges, most)),
        ],
        compiler_params=pltpu.CompilerParams(
            collective_id=0, has_side_effects=True, vmem_limit_bytes=48 * 2**20
        ),
    )(stored, start_block, table, cell)


def solution(mesh):
    placed = (
        P("row", "col", None, None, None),
        P("row", "col", None, None),
        P(("row", "col"), None),
    )
    return jax.shard_map(
        local, mesh=mesh, in_specs=placed, out_specs=(P(("row", "col"), None), P()), check_vma=False
    )
```

```python
import functools

import jax
import jax.numpy as jnp
from jax import lax
from jax.experimental import pallas as pl
from jax.experimental.pallas import tpu as pltpu
from jax.sharding import PartitionSpec as P

EDGE = 128
PANEL = 16
CHAINS = 2
LAG = {"row": 8, "col": 2}
NEAR = 4
FAR_FIRST = True
MESH = pl.DeviceIdType.MESH
HIGH = lax.Precision.HIGHEST
F32 = jnp.float32
BF16 = jnp.bfloat16


def kernel(
    nr, nc, slots, order,
    tiles_hbm, start_hbm, table, cell,
    ritz_ref, gram_ref,
    tiles, start, dense, rbuf, cbuf, scale_r, scale_c,
    sT, w1, w2, w3, w4, x4,
    kept, given, land1, land2, gpart, ga, gs, gb, gfull, elim,
    load_sem, send_sem, recv_sem,
):
    me_of = {"row": lax.axis_index("row"), "col": lax.axis_index("col")}
    me_r, me_c = me_of["row"], me_of["col"]
    size = {"row": nr, "col": nc}
    deep = EDGE // CHAINS
    pending = []

    def lanes(tile):
        return pl.ds(pl.multiple_of(tile * EDGE, EDGE), EDGE)

    def copy(x, axis, peer, src, dst, slot):
        return pltpu.make_async_remote_copy(
            src_ref=src, dst_ref=dst, send_sem=send_sem.at[x], recv_sem=recv_sem.at[x, slot],
            device_id={axis: peer}, device_id_type=MESH,
        )

    def arrived(x, axis, ref, slot):
        copy(x, axis, me_of[axis], ref, ref, slot).wait_recv()

    def sent(x, axis, ref):
        pending.append(lambda: copy(x, axis, me_of[axis], ref, ref, 0).wait_send())

    def flush():
        while pending:
            pending.pop(0)()

    def place(axis):
        me = me_of[axis]
        return size[axis] // 2, me // 2, lax.rem(me, 2), me + 1 - 2 * lax.rem(me, 2)

    def group_at(axis, k):
        groups, mine, _, _ = place(axis)
        return lax.rem(mine + groups // 2 + (k + 1) // 2 * (2 * lax.rem(k, 2) - 1) + groups, groups)

    def others(axis, body):
        @pl.loop(0, size[axis])
        def _(k):
            peer = group_at(axis, k // 2) * 2 + lax.rem(k, 2)

            @pl.when(peer != me_of[axis])
            def _():
                body(peer)

    def send_all(x, axis, src_of, dst):
        others(axis, lambda peer: copy(x, axis, peer, src_of(peer), dst, me_of[axis]).start())

    def wait_all(x, axis, dst_of):
        n, me = size[axis], me_of[axis]

        @pl.loop(1, n)
        def _(k):
            source = lax.rem(me + k, n)
            arrived(x, axis, dst_of(source), source)

    load = pltpu.make_async_copy(tiles_hbm, tiles.at[pl.ds(0, slots)], load_sem.at[0])
    load.start()
    load_start = pltpu.make_async_copy(start_hbm, start, load_sem.at[1])
    load_start.start()
    barrier = pltpu.get_barrier_semaphore()
    for axis in ("row", "col"):
        others(axis, lambda peer, axis=axis: pl.semaphore_signal(
            barrier, inc=1, device_id={axis: peer}, device_id_type=MESH
        ))

    def depth(s):
        return pl.ds(s * deep, deep)

    whole = pl.ds(0, EDGE)
    chains = [depth(s) for s in range(CHAINS)]

    def gather_send(x, axis, rows, tile, w):
        groups, mine, side, partner = place(axis)
        here = w.at[rows, lanes(me_of[axis])]
        w[rows, lanes(me_of[axis])] = tile

        @pl.loop(0, groups - 1)
        def _(k):
            copy(x, axis, group_at(axis, order_of(k, groups)) * 2 + side, here, here, mine).start()

        copy(x, axis, partner, here, here, groups + mine).start()
        sent(x, axis, w.at[rows, pl.ds(0, groups * EDGE)])

    def gather_pass(x, axis, rows, w, begin=0, end=None):
        groups, mine, side, partner = place(axis)
        last = end is None

        @pl.loop(begin, groups - 1 if last else end)
        def _(k):
            g = group_at(axis, order_of(k, groups))
            here = w.at[rows, lanes(g * 2 + side)]
            arrived(x, axis, here, g)
            copy(x + 1, axis, partner, here, here, groups + g).start()

        if last:
            sent(x + 1, axis, w.at[rows, pl.ds(0, (groups - 1) * EDGE)])

    def order_of(k, groups):
        return k if FAR_FIRST else groups - 2 - k

    def gather_wait(x, axis, rows, w):
        groups, mine, side, partner = place(axis)
        arrived(x, axis, w.at[rows, lanes(partner)], groups + mine)

        @pl.loop(0, groups - 1)
        def _(k):
            g = group_at(axis, order_of(k, groups))
            arrived(x + 1, axis, w.at[rows, lanes(g * 2 + 1 - side)], groups + g)

    def give_one(x, axis, rows, which, k):
        groups, mine, side, partner = place(axis)
        g = group_at(axis, k)
        copy(
            x, axis, partner, given.at[which, g, rows, :], land1.at[which, g, rows, :], g
        ).start()

    def multiply(axis, rows, which, w, k):
        groups, mine, side, partner = place(axis)
        g = group_at(axis, k)
        wide = pl.ds(pl.multiple_of(g * 2 * EDGE, 2 * EDGE), 2 * EDGE)
        if axis == "row":
            y = jnp.dot(w[rows, :], dense[:, wide], preferred_element_type=F32)
        else:
            y = lax.dot_general(
                w[rows, :], dense[wide, :], (((1,), (1,)), ((), ())),
                preferred_element_type=F32,
            )
        first, second = y[:, :EDGE], y[:, EDGE:]
        kept[which, g, rows, :] = jnp.where(side == 0, first, second)
        given[which, g, rows, :] = jnp.where(side == 0, second, first)

    def products(x, axis, which, w, ready):
        groups = size[axis] // 2
        lag = min(LAG[axis], groups)
        for s, rows in enumerate(chains):
            ready(s, rows)

            @pl.loop(0, groups)
            def _(k, s=s, rows=rows):
                multiply(axis, rows, which, w, k)
                give_one(x + 2 * s, axis, rows, which, k)
                if lag < groups:
                    @pl.when(k >= lag)
                    def _():
                        pair_sum(x + 2 * s, axis, rows, which, k - lag)

            if lag < groups:
                pair_sums(x + 2 * s, axis, rows, which, groups - lag)
        if lag == groups:
            for s, rows in enumerate(chains):
                pair_sums(x + 2 * s, axis, rows, which, 0)
        products_sent(x, axis, which)

    def joint_product(x, axis, which, w):
        groups = size[axis] // 2

        @pl.loop(0, groups)
        def _(k):
            multiply(axis, whole, which, w, k)
            give_one(x, axis, chains[0], which, k)

        for s, rows in enumerate(chains):
            if s:
                @pl.loop(0, groups)
                def _(k, s=s, rows=rows):
                    give_one(x + 2 * s, axis, rows, which, k)

        for s, rows in enumerate(chains):
            pair_sums(x + 2 * s, axis, rows, which, 0)
        products_sent(x, axis, which)

    def products_sent(x, axis, which):
        groups = size[axis] // 2
        for s, rows in enumerate(chains):
            sent(x + 2 * s, axis, given.at[which, :, rows, :])
            sent(x + 2 * s + 1, axis, kept.at[which, pl.ds(0, groups - 1), rows, :])

    def pair_sums(x, axis, rows, which, begin):
        @pl.loop(begin, size[axis] // 2)
        def _(k):
            pair_sum(x, axis, rows, which, k)

    def pair_sum(x, axis, rows, which, k):
        groups, mine, side, partner = place(axis)
        keep, land = kept.at[which], land1.at[which]
        g = group_at(axis, k)
        arrived(x, axis, land.at[g, rows, :], g)
        keep[g, rows, :] = keep[g, rows, :] + land[g, rows, :]

        @pl.when(k < groups - 1)
        def _():
            copy(
                x + 1, axis, g * 2 + side, keep.at[g, rows, :], land2.at[which, mine, rows, :], mine
            ).start()

    def total_sum(x, axis, rows, which):
        groups, mine, side, partner = place(axis)
        land = land2.at[which]

        def add(k, total):
            g = group_at(axis, groups - 2 - k)
            arrived(x + 1, axis, land.at[g, rows, :], g)
            return total + land[g, rows, :]

        return lax.fori_loop(0, groups - 1, add, kept[which, mine, rows, :])

    tiles[slots] = jnp.zeros((EDGE, EDGE), BF16)
    load_start.wait()
    sT[:, lanes(me_c)] = start[...].astype(F32).T.astype(BF16)
    load.wait()

    def fold(s, total):
        return total + jnp.where(cell[s] == 0, tiles[s], jnp.zeros((EDGE, EDGE), BF16))

    tiles[slots + 1] = lax.fori_loop(0, slots, fold, jnp.zeros((EDGE, EDGE), BF16), unroll=8)

    @pl.loop(0, nc)
    def _(i):
        most = jnp.zeros((EDGE, EDGE), BF16)
        for j in range(nr):
            which = table[i * nr + j]
            if j == 0:
                which = jnp.where(i == 0, slots + 1, which)
            tile = tiles[which]
            most = jnp.maximum(most, jnp.abs(tile))
        rbuf[me_c, pl.ds(i, 1), :] = jnp.max(most.astype(F32).T, axis=0, keepdims=True)

    pl.semaphore_wait(barrier, nr + nc - 2)
    gather_send(0, "col", whole, sT[:, lanes(me_c)], sT)
    send_all(2, "col", lambda peer: rbuf.at[me_c], rbuf.at[me_c])
    sent(2, "col", rbuf.at[pl.ds(0, nc - 1)])

    @pl.loop(0, nr)
    def _(j):
        most = jnp.zeros((EDGE, EDGE), BF16)
        for i in range(nc):
            which = table[i * nr + j]
            if i == 0:
                which = jnp.where(j == 0, slots + 1, which)
            tile = tiles[which]
            dense[i * EDGE:(i + 1) * EDGE, lanes(j)] = tile
            most = jnp.maximum(most, jnp.abs(tile))
        cbuf[me_r, pl.ds(j, 1), :] = jnp.max(most.astype(F32), axis=0, keepdims=True)

    send_all(3, "row", lambda peer: cbuf.at[me_r], cbuf.at[me_r])
    sent(3, "row", cbuf.at[pl.ds(0, nr - 1)])
    gather_pass(0, "col", whole, sT)
    wait_all(2, "col", lambda source: rbuf.at[source])
    scale_r[...] = 1.0 / jnp.sqrt(jnp.max(rbuf[...], axis=0))
    mine_r = scale_r[pl.ds(me_c, 1), :]
    gather_wait(0, "col", whole, sT)
    for t in range(nc):
        here = slice(t * EDGE, (t + 1) * EDGE)
        w1[:, here] = (scale_r[t:t + 1, :] * sT[:, here].astype(F32)).astype(BF16)
    x = 4

    joint_product(x, "row", 0, w1)
    flush()
    wait_all(3, "row", lambda source: cbuf.at[source])
    scale_c[...] = 1.0 / jnp.sqrt(jnp.max(cbuf[...], axis=0))
    mine_c = scale_c[pl.ds(me_r, 1), :]

    def turn(x, axis, which, scale, w, other):
        y = x + 2 * CHAINS
        for s, rows in enumerate(chains):
            tile = (scale * scale * total_sum(x + 2 * s, axis, rows, which)).astype(BF16)
            gather_send(y + 2 * s, axis, rows, tile, w)
        for s, rows in enumerate(chains):
            gather_pass(y + 2 * s, axis, rows, w)
        z = y + 2 * CHAINS
        products(
            z, other, which + 1, w, lambda s, rows: gather_wait(y + 2 * s, axis, rows, w)
        )
        flush()
        return z

    x = turn(x, "row", 0, mine_c, w2, "col")
    x = turn(x, "col", 1, mine_r, w3, "row")
    iterate = mine_c * jnp.concatenate(
        [total_sum(x + 2 * s, "row", rows, 2) for s, rows in enumerate(chains)], axis=0
    )
    x += 2 * CHAINS

    def outer(v):
        return lax.dot_general(
            v, v, (((1,), (1,)), ((), ())), precision=HIGH, preferred_element_type=F32
        )

    share = EDGE // nc

    def strip(p):
        return pl.ds(pl.multiple_of(p * share, share), share)

    def gram_sum(x, which, local, first=None, second=None, third=None):
        part, a, s, b, full = gpart.at[which], ga.at[which], gs.at[which], gb.at[which], gfull.at[which]
        part[...] = local
        send_all(x, "col", lambda peer: part.at[strip(peer)], a.at[me_c])
        sent(x, "col", a.at[pl.ds(0, nc - 1)])
        a[me_c] = part[strip(me_c), :]
        if first:
            first()
        wait_all(x, "col", lambda source: a.at[source])
        mine = jnp.sum(a[...], axis=0)
        s[...] = mine
        send_all(x + 1, "row", lambda peer: s, b.at[me_r])
        sent(x + 1, "row", b.at[pl.ds(0, nr - 1)])
        b[me_r] = mine
        if second:
            second()
        wait_all(x + 1, "row", lambda source: b.at[source])
        full[strip(me_c), :] = jnp.sum(b[...], axis=0) / order
        send_all(x + 2, "col", lambda peer: full.at[strip(me_c)], full.at[strip(me_c)])
        sent(x + 2, "col", a.at[pl.ds(0, nc - 1)])
        if third:
            third()
        wait_all(x + 2, "col", lambda source: full.at[strip(source)])
        return full[...]

    near = NEAR * nr // 16
    gram = gram_sum(
        x, 0, outer(iterate),
        lambda: gather_send(x + 3, "row", whole, iterate, x4),
        lambda: gather_pass(x + 3, "row", whole, x4, 0, near),
        lambda: gather_pass(x + 3, "row", whole, x4, near),
    )
    flush()

    elim[:, :EDGE] = gram
    row_id = lax.broadcasted_iota(jnp.int32, (EDGE, EDGE), 0)
    lane_id = lax.broadcasted_iota(jnp.int32, (EDGE, EDGE), 1)
    elim[:, EDGE:] = jnp.where(row_id == lane_id, 1.0, 0.0)
    lane = lax.broadcasted_iota(jnp.int32, (PANEL, EDGE), 1)
    sub = lax.broadcasted_iota(jnp.int32, (PANEL, EDGE), 0)

    @pl.loop(0, EDGE // PANEL)
    def _(p):
        rows = pl.ds(pl.multiple_of(p * PANEL, PANEL), PANEL)
        left = elim[rows, :EDGE]
        right = elim[rows, EDGE:]
        column = [
            jnp.broadcast_to(
                jnp.sum(jnp.where(lane == p * PANEL + k, left, 0.0), axis=1, keepdims=True),
                (PANEL, EDGE),
            )
            for k in range(PANEL)
        ]
        for k in range(PANEL):
            inv = 1.0 / jnp.sqrt(column[k][k:k + 1, :])
            step = jnp.where(sub > k, column[k] * inv, 0.0)
            l_row = left[k:k + 1, :] * inv
            r_row = right[k:k + 1, :] * inv
            left = jnp.where(sub == k, l_row, left - step * l_row)
            right = jnp.where(sub == k, r_row, right - step * r_row)
            for m in range(k + 1, PANEL):
                column[m] = column[m] - step * (column[m][k:k + 1, :] * inv)
        elim[rows, :EDGE] = left
        elim[rows, EDGE:] = right
        later = jnp.where(lane >= (p + 1) * PANEL, left, 0.0)
        both = jnp.concatenate([left, right], axis=1)
        elim[...] -= lax.dot_general(
            later, both, (((0,), (0,)), ((), ())), precision=HIGH, preferred_element_type=F32
        )

    gather_wait(x + 3, "row", whole, x4)
    inverse = elim[:, EDGE:]
    for t in range(0, nr, 2):
        here = slice(t * EDGE, (t + 2) * EDGE)
        basis = jnp.dot(inverse, x4[:, here], precision=HIGH, preferred_element_type=F32)
        both = jnp.concatenate([scale_c[t:t + 1, :], scale_c[t + 1:t + 2, :]], axis=1)
        w4[:, here] = (both * basis).astype(BF16)
    x += 5
    chains = [whole]
    products(x, "col", 3, w4, lambda s, rows: None)
    ritz = mine_r * total_sum(x, "col", whole, 3)
    x += 2
    ritz_ref[...] = ritz.T
    gram_ref[...] = gram_sum(x, 1, outer(ritz), flush)
    flush()


def local(affinity_tiles, tile_index, start_block):
    nr, nc = lax.axis_size("row"), lax.axis_size("col")
    stored = affinity_tiles[0, 0]
    index = tile_index[0, 0]
    slots = stored.shape[0]
    cell = index[0] * nr + index[1]
    hit = cell[:, None] == jnp.arange(nr * nc, dtype=jnp.int32)[None, :]
    number = jnp.arange(slots, dtype=jnp.int32)[:, None]
    table = jnp.min(jnp.where(hit, number, slots), axis=0)
    most = max(nr, nc)
    groups = most // 2
    share = EDGE // nc
    tile = (EDGE, EDGE)
    exchanges = 14 + 10 * CHAINS
    vmem = pltpu.VMEM
    return pl.pallas_call(
        functools.partial(kernel, nr, nc, slots, nr * nc * EDGE),
        out_shape=(jax.ShapeDtypeStruct(tile, F32), jax.ShapeDtypeStruct(tile, F32)),
        in_specs=[
            pl.BlockSpec(memory_space=pl.ANY),
            pl.BlockSpec(memory_space=pl.ANY),
            pl.BlockSpec(memory_space=pltpu.SMEM),
            pl.BlockSpec(memory_space=pltpu.SMEM),
        ],
        out_specs=(pl.BlockSpec(memory_space=pltpu.VMEM), pl.BlockSpec(memory_space=pltpu.VMEM)),
        scratch_shapes=[
            vmem((slots + 2, *tile), BF16),
            vmem(tile, BF16),
            vmem((nc * EDGE, nr * EDGE), BF16),
            vmem((nc, nc, EDGE), F32),
            vmem((nr, nr, EDGE), F32),
            vmem((nc, EDGE), F32),
            vmem((nr, EDGE), F32),
            vmem((EDGE, nc * EDGE), BF16),
            vmem((EDGE, nc * EDGE), BF16),
            vmem((EDGE, nr * EDGE), BF16),
            vmem((EDGE, nc * EDGE), BF16),
            vmem((EDGE, nr * EDGE), BF16),
            vmem((EDGE, nr * EDGE), F32),
            vmem((4, groups, *tile), F32),
            vmem((4, groups, *tile), F32),
            vmem((4, groups, *tile), F32),
            vmem((4, groups, *tile), F32),
            vmem((2, *tile), F32),
            vmem((2, nc, share, EDGE), F32),
            vmem((2, share, EDGE), F32),
            vmem((2, nr, share, EDGE), F32),
            vmem((2, *tile), F32),
            vmem((EDGE, 2 * EDGE), F32),
            pltpu.SemaphoreType.DMA((2,)),
            pltpu.SemaphoreType.DMA((exchanges,)),
            pltpu.SemaphoreType.DMA((exchanges, most)),
        ],
        compiler_params=pltpu.CompilerParams(
            collective_id=0, has_side_effects=True, vmem_limit_bytes=48 * 2**20
        ),
    )(stored, start_block, table, cell)


def solution(mesh):
    placed = (
        P("row", "col", None, None, None),
        P("row", "col", None, None),
        P(("row", "col"), None),
    )
    return jax.shard_map(
        local, mesh=mesh, in_specs=placed, out_specs=(P(("row", "col"), None), P()), check_vma=False
    )
```

```python
import functools

import jax
import jax.numpy as jnp
from jax import lax
from jax.experimental import pallas as pl
from jax.experimental.pallas import tpu as pltpu
from jax.sharding import PartitionSpec as P

EDGE = 128
PANEL = 16
CHAINS = 2
LAG = {"row": 8, "col": 3}
NEAR = 4
FAR_FIRST = True
MESH = pl.DeviceIdType.MESH
HIGH = lax.Precision.HIGHEST
F32 = jnp.float32
BF16 = jnp.bfloat16


def kernel(
    nr, nc, slots, order,
    tiles_hbm, start_hbm, table, cell,
    ritz_ref, gram_ref,
    tiles, start, dense, rbuf, cbuf, scale_r, scale_c,
    sT, w1, w2, w3, w4, x4,
    kept, given, land1, land2, gpart, ga, gs, gb, gfull, elim,
    load_sem, send_sem, recv_sem,
):
    me_of = {"row": lax.axis_index("row"), "col": lax.axis_index("col")}
    me_r, me_c = me_of["row"], me_of["col"]
    size = {"row": nr, "col": nc}
    deep = EDGE // CHAINS
    pending = []

    def lanes(tile):
        return pl.ds(pl.multiple_of(tile * EDGE, EDGE), EDGE)

    def copy(x, axis, peer, src, dst, slot):
        return pltpu.make_async_remote_copy(
            src_ref=src, dst_ref=dst, send_sem=send_sem.at[x], recv_sem=recv_sem.at[x, slot],
            device_id={axis: peer}, device_id_type=MESH,
        )

    def arrived(x, axis, ref, slot):
        copy(x, axis, me_of[axis], ref, ref, slot).wait_recv()

    def sent(x, axis, ref):
        pending.append(lambda: copy(x, axis, me_of[axis], ref, ref, 0).wait_send())

    def flush():
        while pending:
            pending.pop(0)()

    def place(axis):
        me = me_of[axis]
        return size[axis] // 2, me // 2, lax.rem(me, 2), me + 1 - 2 * lax.rem(me, 2)

    def group_at(axis, k):
        groups, mine, _, _ = place(axis)
        return lax.rem(mine + groups // 2 + (k + 1) // 2 * (2 * lax.rem(k, 2) - 1) + groups, groups)

    def others(axis, body):
        @pl.loop(0, size[axis])
        def _(k):
            peer = group_at(axis, k // 2) * 2 + lax.rem(k, 2)

            @pl.when(peer != me_of[axis])
            def _():
                body(peer)

    def send_all(x, axis, src_of, dst):
        others(axis, lambda peer: copy(x, axis, peer, src_of(peer), dst, me_of[axis]).start())

    def wait_all(x, axis, dst_of):
        n, me = size[axis], me_of[axis]

        @pl.loop(1, n)
        def _(k):
            source = lax.rem(me + k, n)
            arrived(x, axis, dst_of(source), source)

    load = pltpu.make_async_copy(tiles_hbm, tiles.at[pl.ds(0, slots)], load_sem.at[0])
    load.start()
    load_start = pltpu.make_async_copy(start_hbm, start, load_sem.at[1])
    load_start.start()
    barrier = pltpu.get_barrier_semaphore()
    for axis in ("row", "col"):
        others(axis, lambda peer, axis=axis: pl.semaphore_signal(
            barrier, inc=1, device_id={axis: peer}, device_id_type=MESH
        ))

    def depth(s):
        return pl.ds(s * deep, deep)

    whole = pl.ds(0, EDGE)
    chains = [depth(s) for s in range(CHAINS)]

    def gather_send(x, axis, rows, tile, w):
        groups, mine, side, partner = place(axis)
        here = w.at[rows, lanes(me_of[axis])]
        w[rows, lanes(me_of[axis])] = tile

        @pl.loop(0, groups - 1)
        def _(k):
            copy(x, axis, group_at(axis, order_of(k, groups)) * 2 + side, here, here, mine).start()

        copy(x, axis, partner, here, here, groups + mine).start()
        sent(x, axis, w.at[rows, pl.ds(0, groups * EDGE)])

    def gather_pass(x, axis, rows, w, begin=0, end=None):
        groups, mine, side, partner = place(axis)
        last = end is None

        @pl.loop(begin, groups - 1 if last else end)
        def _(k):
            g = group_at(axis, order_of(k, groups))
            here = w.at[rows, lanes(g * 2 + side)]
            arrived(x, axis, here, g)
            copy(x + 1, axis, partner, here, here, groups + g).start()

        if last:
            sent(x + 1, axis, w.at[rows, pl.ds(0, (groups - 1) * EDGE)])

    def order_of(k, groups):
        return k if FAR_FIRST else groups - 2 - k

    def gather_wait(x, axis, rows, w):
        groups, mine, side, partner = place(axis)
        arrived(x, axis, w.at[rows, lanes(partner)], groups + mine)

        @pl.loop(0, groups - 1)
        def _(k):
            g = group_at(axis, order_of(k, groups))
            arrived(x + 1, axis, w.at[rows, lanes(g * 2 + 1 - side)], groups + g)

    def give_one(x, axis, rows, which, k):
        groups, mine, side, partner = place(axis)
        g = group_at(axis, k)
        copy(
            x, axis, partner, given.at[which, g, rows, :], land1.at[which, g, rows, :], g
        ).start()

    def multiply(axis, rows, which, w, k):
        groups, mine, side, partner = place(axis)
        g = group_at(axis, k)
        wide = pl.ds(pl.multiple_of(g * 2 * EDGE, 2 * EDGE), 2 * EDGE)
        if axis == "row":
            y = jnp.dot(w[rows, :], dense[:, wide], preferred_element_type=F32)
        else:
            y = lax.dot_general(
                w[rows, :], dense[wide, :], (((1,), (1,)), ((), ())),
                preferred_element_type=F32,
            )
        first, second = y[:, :EDGE], y[:, EDGE:]
        kept[which, g, rows, :] = jnp.where(side == 0, first, second)
        given[which, g, rows, :] = jnp.where(side == 0, second, first)

    def products(x, axis, which, w, ready):
        groups = size[axis] // 2
        lag = min(LAG[axis], groups)
        for s, rows in enumerate(chains):
            ready(s, rows)

            @pl.loop(0, groups)
            def _(k, s=s, rows=rows):
                multiply(axis, rows, which, w, k)
                give_one(x + 2 * s, axis, rows, which, k)
                if lag < groups:
                    @pl.when(k >= lag)
                    def _():
                        pair_sum(x + 2 * s, axis, rows, which, k - lag)

            if lag < groups:
                pair_sums(x + 2 * s, axis, rows, which, groups - lag)
        if lag == groups:
            for s, rows in enumerate(chains):
                pair_sums(x + 2 * s, axis, rows, which, 0)
        products_sent(x, axis, which)

    def joint_product(x, axis, which, w):
        groups = size[axis] // 2

        @pl.loop(0, groups)
        def _(k):
            multiply(axis, whole, which, w, k)
            give_one(x, axis, chains[0], which, k)

        for s, rows in enumerate(chains):
            if s:
                @pl.loop(0, groups)
                def _(k, s=s, rows=rows):
                    give_one(x + 2 * s, axis, rows, which, k)

        for s, rows in enumerate(chains):
            pair_sums(x + 2 * s, axis, rows, which, 0)
        products_sent(x, axis, which)

    def products_sent(x, axis, which):
        groups = size[axis] // 2
        for s, rows in enumerate(chains):
            sent(x + 2 * s, axis, given.at[which, :, rows, :])
            sent(x + 2 * s + 1, axis, kept.at[which, pl.ds(0, groups - 1), rows, :])

    def pair_sums(x, axis, rows, which, begin):
        @pl.loop(begin, size[axis] // 2)
        def _(k):
            pair_sum(x, axis, rows, which, k)

    def pair_sum(x, axis, rows, which, k):
        groups, mine, side, partner = place(axis)
        keep, land = kept.at[which], land1.at[which]
        g = group_at(axis, k)
        arrived(x, axis, land.at[g, rows, :], g)
        keep[g, rows, :] = keep[g, rows, :] + land[g, rows, :]

        @pl.when(k < groups - 1)
        def _():
            copy(
                x + 1, axis, g * 2 + side, keep.at[g, rows, :], land2.at[which, mine, rows, :], mine
            ).start()

    def total_sum(x, axis, rows, which):
        groups, mine, side, partner = place(axis)
        land = land2.at[which]

        def add(k, total):
            g = group_at(axis, groups - 2 - k)
            arrived(x + 1, axis, land.at[g, rows, :], g)
            return total + land[g, rows, :]

        return lax.fori_loop(0, groups - 1, add, kept[which, mine, rows, :])

    tiles[slots] = jnp.zeros((EDGE, EDGE), BF16)
    load_start.wait()
    sT[:, lanes(me_c)] = start[...].astype(F32).T.astype(BF16)
    load.wait()

    def fold(s, total):
        return total + jnp.where(cell[s] == 0, tiles[s], jnp.zeros((EDGE, EDGE), BF16))

    tiles[slots + 1] = lax.fori_loop(0, slots, fold, jnp.zeros((EDGE, EDGE), BF16), unroll=8)

    @pl.loop(0, nc)
    def _(i):
        most = jnp.zeros((EDGE, EDGE), BF16)
        for j in range(nr):
            which = table[i * nr + j]
            if j == 0:
                which = jnp.where(i == 0, slots + 1, which)
            tile = tiles[which]
            most = jnp.maximum(most, jnp.abs(tile))
        rbuf[me_c, pl.ds(i, 1), :] = jnp.max(most.astype(F32).T, axis=0, keepdims=True)

    pl.semaphore_wait(barrier, nr + nc - 2)
    gather_send(0, "col", whole, sT[:, lanes(me_c)], sT)
    send_all(2, "col", lambda peer: rbuf.at[me_c], rbuf.at[me_c])
    sent(2, "col", rbuf.at[pl.ds(0, nc - 1)])

    @pl.loop(0, nr)
    def _(j):
        most = jnp.zeros((EDGE, EDGE), BF16)
        for i in range(nc):
            which = table[i * nr + j]
            if i == 0:
                which = jnp.where(j == 0, slots + 1, which)
            tile = tiles[which]
            dense[i * EDGE:(i + 1) * EDGE, lanes(j)] = tile
            most = jnp.maximum(most, jnp.abs(tile))
        cbuf[me_r, pl.ds(j, 1), :] = jnp.max(most.astype(F32), axis=0, keepdims=True)

    send_all(3, "row", lambda peer: cbuf.at[me_r], cbuf.at[me_r])
    sent(3, "row", cbuf.at[pl.ds(0, nr - 1)])
    gather_pass(0, "col", whole, sT)
    wait_all(2, "col", lambda source: rbuf.at[source])
    scale_r[...] = 1.0 / jnp.sqrt(jnp.max(rbuf[...], axis=0))
    mine_r = scale_r[pl.ds(me_c, 1), :]
    gather_wait(0, "col", whole, sT)
    for t in range(nc):
        here = slice(t * EDGE, (t + 1) * EDGE)
        w1[:, here] = (scale_r[t:t + 1, :] * sT[:, here].astype(F32)).astype(BF16)
    x = 4

    joint_product(x, "row", 0, w1)
    flush()
    wait_all(3, "row", lambda source: cbuf.at[source])
    scale_c[...] = 1.0 / jnp.sqrt(jnp.max(cbuf[...], axis=0))
    mine_c = scale_c[pl.ds(me_r, 1), :]

    def turn(x, axis, which, scale, w, other):
        y = x + 2 * CHAINS
        for s, rows in enumerate(chains):
            tile = (scale * scale * total_sum(x + 2 * s, axis, rows, which)).astype(BF16)
            gather_send(y + 2 * s, axis, rows, tile, w)
        for s, rows in enumerate(chains):
            gather_pass(y + 2 * s, axis, rows, w)
        z = y + 2 * CHAINS
        products(
            z, other, which + 1, w, lambda s, rows: gather_wait(y + 2 * s, axis, rows, w)
        )
        flush()
        return z

    x = turn(x, "row", 0, mine_c, w2, "col")
    x = turn(x, "col", 1, mine_r, w3, "row")
    iterate = mine_c * jnp.concatenate(
        [total_sum(x + 2 * s, "row", rows, 2) for s, rows in enumerate(chains)], axis=0
    )
    x += 2 * CHAINS

    def outer(v):
        return lax.dot_general(
            v, v, (((1,), (1,)), ((), ())), precision=HIGH, preferred_element_type=F32
        )

    share = EDGE // nc

    def strip(p):
        return pl.ds(pl.multiple_of(p * share, share), share)

    def gram_sum(x, which, local, first=None, second=None, third=None):
        part, a, s, b, full = gpart.at[which], ga.at[which], gs.at[which], gb.at[which], gfull.at[which]
        part[...] = local
        send_all(x, "col", lambda peer: part.at[strip(peer)], a.at[me_c])
        sent(x, "col", a.at[pl.ds(0, nc - 1)])
        a[me_c] = part[strip(me_c), :]
        if first:
            first()
        wait_all(x, "col", lambda source: a.at[source])
        mine = jnp.sum(a[...], axis=0)
        s[...] = mine
        send_all(x + 1, "row", lambda peer: s, b.at[me_r])
        sent(x + 1, "row", b.at[pl.ds(0, nr - 1)])
        b[me_r] = mine
        if second:
            second()
        wait_all(x + 1, "row", lambda source: b.at[source])
        full[strip(me_c), :] = jnp.sum(b[...], axis=0) / order
        send_all(x + 2, "col", lambda peer: full.at[strip(me_c)], full.at[strip(me_c)])
        sent(x + 2, "col", a.at[pl.ds(0, nc - 1)])
        if third:
            third()
        wait_all(x + 2, "col", lambda source: full.at[strip(source)])
        return full[...]

    near = NEAR * nr // 16
    gram = gram_sum(
        x, 0, outer(iterate),
        lambda: gather_send(x + 3, "row", whole, iterate, x4),
        lambda: gather_pass(x + 3, "row", whole, x4, 0, near),
        lambda: gather_pass(x + 3, "row", whole, x4, near),
    )
    flush()

    elim[:, :EDGE] = gram
    row_id = lax.broadcasted_iota(jnp.int32, (EDGE, EDGE), 0)
    lane_id = lax.broadcasted_iota(jnp.int32, (EDGE, EDGE), 1)
    elim[:, EDGE:] = jnp.where(row_id == lane_id, 1.0, 0.0)
    lane = lax.broadcasted_iota(jnp.int32, (PANEL, EDGE), 1)
    sub = lax.broadcasted_iota(jnp.int32, (PANEL, EDGE), 0)

    @pl.loop(0, EDGE // PANEL)
    def _(p):
        rows = pl.ds(pl.multiple_of(p * PANEL, PANEL), PANEL)
        left = elim[rows, :EDGE]
        right = elim[rows, EDGE:]
        column = [
            jnp.broadcast_to(
                jnp.sum(jnp.where(lane == p * PANEL + k, left, 0.0), axis=1, keepdims=True),
                (PANEL, EDGE),
            )
            for k in range(PANEL)
        ]
        for k in range(PANEL):
            inv = 1.0 / jnp.sqrt(column[k][k:k + 1, :])
            step = jnp.where(sub > k, column[k] * inv, 0.0)
            l_row = left[k:k + 1, :] * inv
            r_row = right[k:k + 1, :] * inv
            left = jnp.where(sub == k, l_row, left - step * l_row)
            right = jnp.where(sub == k, r_row, right - step * r_row)
            for m in range(k + 1, PANEL):
                column[m] = column[m] - step * (column[m][k:k + 1, :] * inv)
        elim[rows, :EDGE] = left
        elim[rows, EDGE:] = right
        later = jnp.where(lane >= (p + 1) * PANEL, left, 0.0)
        both = jnp.concatenate([left, right], axis=1)
        elim[...] -= lax.dot_general(
            later, both, (((0,), (0,)), ((), ())), precision=HIGH, preferred_element_type=F32
        )

    gather_wait(x + 3, "row", whole, x4)
    inverse = elim[:, EDGE:]
    for t in range(0, nr, 2):
        here = slice(t * EDGE, (t + 2) * EDGE)
        basis = jnp.dot(inverse, x4[:, here], precision=HIGH, preferred_element_type=F32)
        both = jnp.concatenate([scale_c[t:t + 1, :], scale_c[t + 1:t + 2, :]], axis=1)
        w4[:, here] = (both * basis).astype(BF16)
    x += 5
    chains = [whole]
    products(x, "col", 3, w4, lambda s, rows: None)
    ritz = mine_r * total_sum(x, "col", whole, 3)
    x += 2
    ritz_ref[...] = ritz.T
    gram_ref[...] = gram_sum(x, 1, outer(ritz), flush)
    flush()


def local(affinity_tiles, tile_index, start_block):
    nr, nc = lax.axis_size("row"), lax.axis_size("col")
    stored = affinity_tiles[0, 0]
    index = tile_index[0, 0]
    slots = stored.shape[0]
    cell = index[0] * nr + index[1]
    hit = cell[:, None] == jnp.arange(nr * nc, dtype=jnp.int32)[None, :]
    number = jnp.arange(slots, dtype=jnp.int32)[:, None]
    table = jnp.min(jnp.where(hit, number, slots), axis=0)
    most = max(nr, nc)
    groups = most // 2
    share = EDGE // nc
    tile = (EDGE, EDGE)
    exchanges = 14 + 10 * CHAINS
    vmem = pltpu.VMEM
    return pl.pallas_call(
        functools.partial(kernel, nr, nc, slots, nr * nc * EDGE),
        out_shape=(jax.ShapeDtypeStruct(tile, F32), jax.ShapeDtypeStruct(tile, F32)),
        in_specs=[
            pl.BlockSpec(memory_space=pl.ANY),
            pl.BlockSpec(memory_space=pl.ANY),
            pl.BlockSpec(memory_space=pltpu.SMEM),
            pl.BlockSpec(memory_space=pltpu.SMEM),
        ],
        out_specs=(pl.BlockSpec(memory_space=pltpu.VMEM), pl.BlockSpec(memory_space=pltpu.VMEM)),
        scratch_shapes=[
            vmem((slots + 2, *tile), BF16),
            vmem(tile, BF16),
            vmem((nc * EDGE, nr * EDGE), BF16),
            vmem((nc, nc, EDGE), F32),
            vmem((nr, nr, EDGE), F32),
            vmem((nc, EDGE), F32),
            vmem((nr, EDGE), F32),
            vmem((EDGE, nc * EDGE), BF16),
            vmem((EDGE, nc * EDGE), BF16),
            vmem((EDGE, nr * EDGE), BF16),
            vmem((EDGE, nc * EDGE), BF16),
            vmem((EDGE, nr * EDGE), BF16),
            vmem((EDGE, nr * EDGE), F32),
            vmem((4, groups, *tile), F32),
            vmem((4, groups, *tile), F32),
            vmem((4, groups, *tile), F32),
            vmem((4, groups, *tile), F32),
            vmem((2, *tile), F32),
            vmem((2, nc, share, EDGE), F32),
            vmem((2, share, EDGE), F32),
            vmem((2, nr, share, EDGE), F32),
            vmem((2, *tile), F32),
            vmem((EDGE, 2 * EDGE), F32),
            pltpu.SemaphoreType.DMA((2,)),
            pltpu.SemaphoreType.DMA((exchanges,)),
            pltpu.SemaphoreType.DMA((exchanges, most)),
        ],
        compiler_params=pltpu.CompilerParams(
            collective_id=0, has_side_effects=True, vmem_limit_bytes=48 * 2**20
        ),
    )(stored, start_block, table, cell)


def solution(mesh):
    placed = (
        P("row", "col", None, None, None),
        P("row", "col", None, None),
        P(("row", "col"), None),
    )
    return jax.shard_map(
        local, mesh=mesh, in_specs=placed, out_specs=(P(("row", "col"), None), P()), check_vma=False
    )
```

```python
import functools

import jax
import jax.numpy as jnp
from jax import lax
from jax.experimental import pallas as pl
from jax.experimental.pallas import tpu as pltpu
from jax.sharding import PartitionSpec as P

EDGE = 128
PANEL = 16
CHAINS = 2
LAG = {"row": 8, "col": 3}
NEAR = 4
FAR_FIRST = True
MESH = pl.DeviceIdType.MESH
HIGH = lax.Precision.HIGHEST
F32 = jnp.float32
BF16 = jnp.bfloat16


def kernel(
    nr, nc, slots, order,
    tiles_hbm, start_hbm, table, cell,
    ritz_ref, gram_ref,
    tiles, start, dense, rbuf, cbuf, scale_r, scale_c,
    sT, w1, w2, w3, w4, x4,
    kept, given, land1, land2, gpart, ga, gs, gb, gfull, elim,
    load_sem, send_sem, recv_sem,
):
    me_of = {"row": lax.axis_index("row"), "col": lax.axis_index("col")}
    me_r, me_c = me_of["row"], me_of["col"]
    size = {"row": nr, "col": nc}
    deep = EDGE // CHAINS
    pending = []

    def lanes(tile):
        return pl.ds(pl.multiple_of(tile * EDGE, EDGE), EDGE)

    def copy(x, axis, peer, src, dst, slot):
        return pltpu.make_async_remote_copy(
            src_ref=src, dst_ref=dst, send_sem=send_sem.at[x], recv_sem=recv_sem.at[x, slot],
            device_id={axis: peer}, device_id_type=MESH,
        )

    def arrived(x, axis, ref, slot):
        copy(x, axis, me_of[axis], ref, ref, slot).wait_recv()

    def sent(x, axis, ref):
        pending.append(lambda: copy(x, axis, me_of[axis], ref, ref, 0).wait_send())

    def flush():
        while pending:
            pending.pop(0)()

    def place(axis):
        me = me_of[axis]
        return size[axis] // 2, me // 2, lax.rem(me, 2), me + 1 - 2 * lax.rem(me, 2)

    def group_at(axis, k):
        groups, mine, _, _ = place(axis)
        return lax.rem(mine + groups // 2 + (k + 1) // 2 * (2 * lax.rem(k, 2) - 1) + groups, groups)

    def others(axis, body):
        @pl.loop(0, size[axis])
        def _(k):
            peer = group_at(axis, k // 2) * 2 + lax.rem(k, 2)

            @pl.when(peer != me_of[axis])
            def _():
                body(peer)

    def send_all(x, axis, src_of, dst):
        others(axis, lambda peer: copy(x, axis, peer, src_of(peer), dst, me_of[axis]).start())

    def wait_all(x, axis, dst_of):
        n, me = size[axis], me_of[axis]

        @pl.loop(1, n)
        def _(k):
            source = lax.rem(me + k, n)
            arrived(x, axis, dst_of(source), source)

    load = pltpu.make_async_copy(tiles_hbm, tiles.at[pl.ds(0, slots)], load_sem.at[0])
    load.start()
    load_start = pltpu.make_async_copy(start_hbm, start, load_sem.at[1])
    load_start.start()
    barrier = pltpu.get_barrier_semaphore()
    for axis in ("row", "col"):
        others(axis, lambda peer, axis=axis: pl.semaphore_signal(
            barrier, inc=1, device_id={axis: peer}, device_id_type=MESH
        ))

    def depth(s):
        return pl.ds(s * deep, deep)

    whole = pl.ds(0, EDGE)
    chains = [depth(s) for s in range(CHAINS)]

    def gather_send(x, axis, rows, tile, w):
        groups, mine, side, partner = place(axis)
        here = w.at[rows, lanes(me_of[axis])]
        w[rows, lanes(me_of[axis])] = tile

        @pl.loop(0, groups - 1)
        def _(k):
            copy(x, axis, group_at(axis, order_of(k, groups)) * 2 + side, here, here, mine).start()

        copy(x, axis, partner, here, here, groups + mine).start()
        sent(x, axis, w.at[rows, pl.ds(0, groups * EDGE)])

    def gather_pass(x, axis, rows, w, begin=0, end=None):
        groups, mine, side, partner = place(axis)
        last = end is None

        @pl.loop(begin, groups - 1 if last else end)
        def _(k):
            g = group_at(axis, order_of(k, groups))
            here = w.at[rows, lanes(g * 2 + side)]
            arrived(x, axis, here, g)
            copy(x + 1, axis, partner, here, here, groups + g).start()

        if last:
            sent(x + 1, axis, w.at[rows, pl.ds(0, (groups - 1) * EDGE)])

    def order_of(k, groups):
        return k if FAR_FIRST else groups - 2 - k

    def gather_wait(x, axis, rows, w):
        groups, mine, side, partner = place(axis)
        arrived(x, axis, w.at[rows, lanes(partner)], groups + mine)

        @pl.loop(0, groups - 1)
        def _(k):
            g = group_at(axis, order_of(k, groups))
            arrived(x + 1, axis, w.at[rows, lanes(g * 2 + 1 - side)], groups + g)

    def give_one(x, axis, rows, which, k):
        groups, mine, side, partner = place(axis)
        g = group_at(axis, k)
        copy(
            x, axis, partner, given.at[which, g, rows, :], land1.at[which, g, rows, :], g
        ).start()

    def multiply(axis, rows, which, w, k):
        groups, mine, side, partner = place(axis)
        g = group_at(axis, k)
        wide = pl.ds(pl.multiple_of(g * 2 * EDGE, 2 * EDGE), 2 * EDGE)
        if axis == "row":
            y = jnp.dot(w[rows, :], dense[:, wide], preferred_element_type=F32)
        else:
            y = lax.dot_general(
                w[rows, :], dense[wide, :], (((1,), (1,)), ((), ())),
                preferred_element_type=F32,
            )
        first, second = y[:, :EDGE], y[:, EDGE:]
        kept[which, g, rows, :] = jnp.where(side == 0, first, second)
        given[which, g, rows, :] = jnp.where(side == 0, second, first)

    def products(x, axis, which, w, ready):
        groups = size[axis] // 2
        lag = min(LAG[axis], groups)
        for s, rows in enumerate(chains):
            ready(s, rows)

            @pl.loop(0, groups)
            def _(k, s=s, rows=rows):
                multiply(axis, rows, which, w, k)
                give_one(x + 2 * s, axis, rows, which, k)
                if lag < groups:
                    @pl.when(k >= lag)
                    def _():
                        pair_sum(x + 2 * s, axis, rows, which, k - lag)

            if lag < groups:
                pair_sums(x + 2 * s, axis, rows, which, groups - lag)
        if lag == groups:
            for s, rows in enumerate(chains):
                pair_sums(x + 2 * s, axis, rows, which, 0)
        products_sent(x, axis, which)

    def joint_product(x, axis, which, w):
        groups = size[axis] // 2

        @pl.loop(0, groups)
        def _(k):
            multiply(axis, whole, which, w, k)
            give_one(x, axis, chains[0], which, k)

        for s, rows in enumerate(chains):
            if s:
                @pl.loop(0, groups)
                def _(k, s=s, rows=rows):
                    give_one(x + 2 * s, axis, rows, which, k)

        for s, rows in enumerate(chains):
            pair_sums(x + 2 * s, axis, rows, which, 0)
        products_sent(x, axis, which)

    def products_sent(x, axis, which):
        groups = size[axis] // 2
        for s, rows in enumerate(chains):
            sent(x + 2 * s, axis, given.at[which, :, rows, :])
            sent(x + 2 * s + 1, axis, kept.at[which, pl.ds(0, groups - 1), rows, :])

    def pair_sums(x, axis, rows, which, begin):
        @pl.loop(begin, size[axis] // 2)
        def _(k):
            pair_sum(x, axis, rows, which, k)

    def pair_sum(x, axis, rows, which, k):
        groups, mine, side, partner = place(axis)
        keep, land = kept.at[which], land1.at[which]
        g = group_at(axis, k)
        arrived(x, axis, land.at[g, rows, :], g)
        keep[g, rows, :] = keep[g, rows, :] + land[g, rows, :]

        @pl.when(k < groups - 1)
        def _():
            copy(
                x + 1, axis, g * 2 + side, keep.at[g, rows, :], land2.at[which, mine, rows, :], mine
            ).start()

    def total_sum(x, axis, rows, which):
        groups, mine, side, partner = place(axis)
        land = land2.at[which]

        def add(k, total):
            g = group_at(axis, groups - 2 - k)
            arrived(x + 1, axis, land.at[g, rows, :], g)
            return total + land[g, rows, :]

        return lax.fori_loop(0, groups - 1, add, kept[which, mine, rows, :])

    tiles[slots] = jnp.zeros((EDGE, EDGE), BF16)
    load_start.wait()
    sT[:, lanes(me_c)] = start[...].astype(F32).T.astype(BF16)
    load.wait()

    def fold(s, total):
        return total + jnp.where(cell[s] == 0, tiles[s], jnp.zeros((EDGE, EDGE), BF16))

    tiles[slots + 1] = lax.fori_loop(0, slots, fold, jnp.zeros((EDGE, EDGE), BF16), unroll=8)

    @pl.loop(0, nc)
    def _(i):
        most = jnp.zeros((EDGE, EDGE), BF16)
        for j in range(nr):
            which = table[i * nr + j]
            if j == 0:
                which = jnp.where(i == 0, slots + 1, which)
            tile = tiles[which]
            most = jnp.maximum(most, jnp.abs(tile))
        rbuf[me_c, pl.ds(i, 1), :] = jnp.max(most.astype(F32).T, axis=0, keepdims=True)

    pl.semaphore_wait(barrier, nr + nc - 2)
    gather_send(0, "col", whole, sT[:, lanes(me_c)], sT)
    send_all(2, "col", lambda peer: rbuf.at[me_c], rbuf.at[me_c])
    sent(2, "col", rbuf.at[pl.ds(0, nc - 1)])

    @pl.loop(0, nr)
    def _(j):
        most = jnp.zeros((EDGE, EDGE), BF16)
        for i in range(nc):
            which = table[i * nr + j]
            if i == 0:
                which = jnp.where(j == 0, slots + 1, which)
            tile = tiles[which]
            dense[i * EDGE:(i + 1) * EDGE, lanes(j)] = tile
            most = jnp.maximum(most, jnp.abs(tile))
        cbuf[me_r, pl.ds(j, 1), :] = jnp.max(most.astype(F32), axis=0, keepdims=True)

    send_all(3, "row", lambda peer: cbuf.at[me_r], cbuf.at[me_r])
    sent(3, "row", cbuf.at[pl.ds(0, nr - 1)])
    gather_pass(0, "col", whole, sT)
    wait_all(2, "col", lambda source: rbuf.at[source])
    scale_r[...] = 1.0 / jnp.sqrt(jnp.max(rbuf[...], axis=0))
    mine_r = scale_r[pl.ds(me_c, 1), :]
    gather_wait(0, "col", whole, sT)
    for t in range(nc):
        here = slice(t * EDGE, (t + 1) * EDGE)
        w1[:, here] = (scale_r[t:t + 1, :] * sT[:, here].astype(F32)).astype(BF16)
    x = 4

    joint_product(x, "row", 0, w1)
    flush()
    wait_all(3, "row", lambda source: cbuf.at[source])
    scale_c[...] = 1.0 / jnp.sqrt(jnp.max(cbuf[...], axis=0))
    mine_c = scale_c[pl.ds(me_r, 1), :]

    def turn(x, axis, which, scale, w, other):
        y = x + 2 * CHAINS
        for s, rows in enumerate(chains):
            tile = (scale * scale * total_sum(x + 2 * s, axis, rows, which)).astype(BF16)
            gather_send(y + 2 * s, axis, rows, tile, w)
        for s, rows in enumerate(chains):
            gather_pass(y + 2 * s, axis, rows, w)
        z = y + 2 * CHAINS
        products(
            z, other, which + 1, w, lambda s, rows: gather_wait(y + 2 * s, axis, rows, w)
        )
        flush()
        return z

    x = turn(x, "row", 0, mine_c, w2, "col")
    x = turn(x, "col", 1, mine_r, w3, "row")
    iterate = mine_c * jnp.concatenate(
        [total_sum(x + 2 * s, "row", rows, 2) for s, rows in enumerate(chains)], axis=0
    )
    x += 2 * CHAINS

    def outer(v):
        return lax.dot_general(
            v, v, (((1,), (1,)), ((), ())), precision=HIGH, preferred_element_type=F32
        )

    share = EDGE // nc

    def strip(p):
        return pl.ds(pl.multiple_of(p * share, share), share)

    def gram_sum(x, which, local, first=None, second=None, third=None):
        part, a, s, b, full = gpart.at[which], ga.at[which], gs.at[which], gb.at[which], gfull.at[which]
        part[...] = local
        send_all(x, "col", lambda peer: part.at[strip(peer)], a.at[me_c])
        sent(x, "col", a.at[pl.ds(0, nc - 1)])
        a[me_c] = part[strip(me_c), :]
        if first:
            first()
        wait_all(x, "col", lambda source: a.at[source])
        mine = jnp.sum(a[...], axis=0)
        s[...] = mine
        send_all(x + 1, "row", lambda peer: s, b.at[me_r])
        sent(x + 1, "row", b.at[pl.ds(0, nr - 1)])
        b[me_r] = mine
        if second:
            second()
        wait_all(x + 1, "row", lambda source: b.at[source])
        full[strip(me_c), :] = jnp.sum(b[...], axis=0) / order
        send_all(x + 2, "col", lambda peer: full.at[strip(me_c)], full.at[strip(me_c)])
        sent(x + 2, "col", a.at[pl.ds(0, nc - 1)])
        if third:
            third()
        wait_all(x + 2, "col", lambda source: full.at[strip(source)])
        return full[...]

    near = NEAR * nr // 16
    gram = gram_sum(
        x, 0, outer(iterate),
        lambda: gather_send(x + 3, "row", whole, iterate, x4),
        lambda: gather_pass(x + 3, "row", whole, x4, 0, near),
        lambda: gather_pass(x + 3, "row", whole, x4, near),
    )
    flush()

    elim[:, :EDGE] = gram
    row_id = lax.broadcasted_iota(jnp.int32, (EDGE, EDGE), 0)
    lane_id = lax.broadcasted_iota(jnp.int32, (EDGE, EDGE), 1)
    elim[:, EDGE:] = jnp.where(row_id == lane_id, 1.0, 0.0)
    lane = lax.broadcasted_iota(jnp.int32, (PANEL, EDGE), 1)
    sub = lax.broadcasted_iota(jnp.int32, (PANEL, EDGE), 0)

    @pl.loop(0, EDGE // PANEL)
    def _(p):
        rows = pl.ds(pl.multiple_of(p * PANEL, PANEL), PANEL)
        left = elim[rows, :EDGE]
        right = elim[rows, EDGE:]
        column = [
            jnp.broadcast_to(
                jnp.sum(jnp.where(lane == p * PANEL + k, left, 0.0), axis=1, keepdims=True),
                (PANEL, EDGE),
            )
            for k in range(PANEL)
        ]
        for k in range(PANEL):
            inv = 1.0 / jnp.sqrt(column[k][k:k + 1, :])
            step = jnp.where(sub > k, column[k] * inv, 0.0)
            l_row = left[k:k + 1, :] * inv
            r_row = right[k:k + 1, :] * inv
            left = jnp.where(sub == k, l_row, left - step * l_row)
            right = jnp.where(sub == k, r_row, right - step * r_row)
            for m in range(k + 1, PANEL):
                column[m] = column[m] - step * (column[m][k:k + 1, :] * inv)
        elim[rows, :EDGE] = left
        elim[rows, EDGE:] = right
        later = jnp.where(lane >= (p + 1) * PANEL, left, 0.0)
        both = jnp.concatenate([left, right], axis=1)
        elim[...] -= lax.dot_general(
            later, both, (((0,), (0,)), ((), ())), precision=HIGH, preferred_element_type=F32
        )

    gather_wait(x + 3, "row", whole, x4)
    inverse = elim[:, EDGE:]
    for t in range(0, nr, 4):
        here = slice(t * EDGE, (t + 4) * EDGE)
        basis = jnp.dot(inverse, x4[:, here], precision=HIGH, preferred_element_type=F32)
        both = jnp.concatenate([scale_c[t + i:t + i + 1, :] for i in range(4)], axis=1)
        w4[:, here] = (both * basis).astype(BF16)
    x += 5
    chains = [whole]
    products(x, "col", 3, w4, lambda s, rows: None)
    ritz = mine_r * total_sum(x, "col", whole, 3)
    x += 2

    def finish():
        ritz_ref[...] = ritz.T
        flush()

    gram_ref[...] = gram_sum(x, 1, outer(ritz), finish)
    flush()


def local(affinity_tiles, tile_index, start_block):
    nr, nc = lax.axis_size("row"), lax.axis_size("col")
    stored = affinity_tiles[0, 0]
    index = tile_index[0, 0]
    slots = stored.shape[0]
    cell = index[0] * nr + index[1]
    hit = cell[:, None] == jnp.arange(nr * nc, dtype=jnp.int32)[None, :]
    number = jnp.arange(slots, dtype=jnp.int32)[:, None]
    table = jnp.min(jnp.where(hit, number, slots), axis=0)
    most = max(nr, nc)
    groups = most // 2
    share = EDGE // nc
    tile = (EDGE, EDGE)
    exchanges = 14 + 10 * CHAINS
    vmem = pltpu.VMEM
    return pl.pallas_call(
        functools.partial(kernel, nr, nc, slots, nr * nc * EDGE),
        out_shape=(jax.ShapeDtypeStruct(tile, F32), jax.ShapeDtypeStruct(tile, F32)),
        in_specs=[
            pl.BlockSpec(memory_space=pl.ANY),
            pl.BlockSpec(memory_space=pl.ANY),
            pl.BlockSpec(memory_space=pltpu.SMEM),
            pl.BlockSpec(memory_space=pltpu.SMEM),
        ],
        out_specs=(pl.BlockSpec(memory_space=pltpu.VMEM), pl.BlockSpec(memory_space=pltpu.VMEM)),
        scratch_shapes=[
            vmem((slots + 2, *tile), BF16),
            vmem(tile, BF16),
            vmem((nc * EDGE, nr * EDGE), BF16),
            vmem((nc, nc, EDGE), F32),
            vmem((nr, nr, EDGE), F32),
            vmem((nc, EDGE), F32),
            vmem((nr, EDGE), F32),
            vmem((EDGE, nc * EDGE), BF16),
            vmem((EDGE, nc * EDGE), BF16),
            vmem((EDGE, nr * EDGE), BF16),
            vmem((EDGE, nc * EDGE), BF16),
            vmem((EDGE, nr * EDGE), BF16),
            vmem((EDGE, nr * EDGE), F32),
            vmem((4, groups, *tile), F32),
            vmem((4, groups, *tile), F32),
            vmem((4, groups, *tile), F32),
            vmem((4, groups, *tile), F32),
            vmem((2, *tile), F32),
            vmem((2, nc, share, EDGE), F32),
            vmem((2, share, EDGE), F32),
            vmem((2, nr, share, EDGE), F32),
            vmem((2, *tile), F32),
            vmem((EDGE, 2 * EDGE), F32),
            pltpu.SemaphoreType.DMA((2,)),
            pltpu.SemaphoreType.DMA((exchanges,)),
            pltpu.SemaphoreType.DMA((exchanges, most)),
        ],
        compiler_params=pltpu.CompilerParams(
            collective_id=0, has_side_effects=True, vmem_limit_bytes=48 * 2**20
        ),
    )(stored, start_block, table, cell)


def solution(mesh):
    placed = (
        P("row", "col", None, None, None),
        P("row", "col", None, None),
        P(("row", "col"), None),
    )
    return jax.shard_map(
        local, mesh=mesh, in_specs=placed, out_specs=(P(("row", "col"), None), P()), check_vma=False
    )
```
